512 devices in a mesh: freq: 16 (over z, y_hi), strip: 32 (over x, y_lo, core).
Axes of the slice: x: 4, y: 8 (y_hi: 2, y_lo: 4; y = y_hi * 4 + y_lo), z: 8, core: 2. Of those that a mesh axis runs over, the one named last changes fastest.
Arguments:
- receiver_field: float32 [2, 16, 256, 2048], P(None, 'freq', 'strip'), may hold values from -17 to 17
- source_field: float32 [2, 16, 256, 2048], P(None, 'freq', 'strip'), may hold values from -4 to 4
- velocity_class: int32 [256, 2048], P('strip'), may hold values from 0 to 7
- filters: float32 [16, 8, 2, 9], P('freq'), may hold values from -0.8 to 0.8
- point_spread: float32 [16, 2, 15, 15], replicated, may hold values from -0.05 to 1
- spread_index: int32 [32, 16], replicated, may hold values from 0 to 15
Outputs:
- migrated: float32 [256, 2, 2048], P('strip', None, 'freq')
- reflectivity: float32 [256, 2, 2048], P('strip', None, 'freq')
- misfit: float32 [], replicated
The draws below stay inside these ranges and needn't reach their ends.
All inputs are finite; a program needn't handle non-finite values.
Results may differ from the reference program's by a relative error of at most 0.0003.
Values sent between devices are 32-bit elements; how exact they have to be, the bound alone decides.
No kernel may reach another device: no remote copies, remote signals or barrier semaphores. Data moves between devices by JAX's collectives and lax.ppermute only.
A program may use at most 64 MiB of HBM per device.

```python
import math
import jax
import jax.numpy as jnp
from jax import lax

ROWS = 8
BCOLS = 128
STEPS = 2
NCLASS = 8
PSF_SIDE = 15
NPSF = 16
PASSES = 2
NX = 256
NY = 2048
NF = 16
BRICKS_X = 32
BRICKS_Y = 16


def draw_receiver_field(key, part):
    shape = (2, NF, NX, NY)
    across = jnp.arange(NY, dtype=jnp.float32) / NY
    raw = jax.random.truncated_normal(key, -4.0, 4.0, shape, jnp.float32)
    return raw * jnp.power(3.0, across)[None, None, None, :]


def draw_filters(key, part):
    first, second, third = jax.random.split(jax.random.fold_in(key, 17), 3)
    shape = (NF, NCLASS, 2, 9)
    taps = 0.15 * jax.random.truncated_normal(first, -4.0, 4.0, shape, jnp.float32)
    phase = jax.random.uniform(second, (NF, NCLASS), jnp.float32, -math.pi, math.pi)
    length = jax.random.uniform(third, (NF, NCLASS), jnp.float32, 0.6, 0.8)
    center = jnp.stack([length * jnp.cos(phase), length * jnp.sin(phase)], axis=2)
    return taps.at[:, :, :, 4].set(center)


def draw_point_spread(key, part):
    first, second = jax.random.split(jax.random.fold_in(key, 29), 2)
    shape = (NPSF, STEPS, PSF_SIDE, PSF_SIDE)
    raw = 0.012 * jax.random.truncated_normal(first, -4.0, 4.0, shape, jnp.float32)
    center = jax.random.uniform(second, (NPSF,), jnp.float32, 0.8, 1.0)
    return raw.at[:, 0, PSF_SIDE // 2, PSF_SIDE // 2].set(center)


def with_ends(array, own_key, low, top_value):
    longest = array.shape.index(max(array.shape))
    spots = []
    for shift in (0, 1):
        where = [jax.random.randint(jax.random.fold_in(own_key, axis), (), 0, length) for axis, length in enumerate(array.shape)]
        where[longest] = (where[longest] + shift) % array.shape[longest]
        spots.append(tuple(where))
    return array.at[spots[0]].set(low).at[spots[1]].set(top_value)


def block_scale(rng, extent, shards, smallest, top_value):
    def one(position, shards_of):
        steps = jax.random.uniform(jax.random.fold_in(jax.random.fold_in(rng, 6), position), (shards_of,), jnp.float32, smallest / len(shards), top_value / len(shards))
        return jnp.repeat(jnp.exp(steps), extent[position] // shards_of).reshape((-1,) + (1,) * (len(extent) - position - 1))

    factor_of = one(*shards[0])
    for cut in shards[1:]:
        factor_of = factor_of * one(*cut)
    return factor_of


def bell_draw(own_key, dims, spread, most, pieces=(), held_as=jnp.bfloat16):
    entries = jax.random.normal(own_key, dims, jnp.float32) * spread
    if len(pieces) > 0:
        entries = block_scale(own_key, dims, pieces, -0.22, 0.18) * entries
    return jnp.clip(entries, min=-most, max=most).astype(held_as)


def setup_inputs(seed: int = 0) -> dict:
    keys = jax.random.split(jax.random.key(seed), 7)
    return {
        "receiver_field": draw_receiver_field(jax.random.fold_in(keys[6], 71), 0),
        "source_field": bell_draw(keys[1], (2, NF, NX, NY), 1.0, 4.0, ((1, 16), (2, 32)), jnp.float32),
        "velocity_class": with_ends(jax.random.randint(keys[2], (NX, NY), 0, NCLASS), jax.random.fold_in(keys[2], 1), 0, NCLASS - 1).astype(jnp.int32),
        "filters": draw_filters(jax.random.fold_in(keys[6], 71), 0),
        "point_spread": draw_point_spread(jax.random.fold_in(keys[6], 71), 0),
        "spread_index": with_ends(jax.random.randint(keys[5], (BRICKS_X, BRICKS_Y), 0, NPSF), jax.random.fold_in(keys[5], 1), 0, NPSF - 1).astype(jnp.int32),
    }


HIGHEST = lax.Precision.HIGHEST

def advance(wavefield, velocity_class, filters_now, factor):
    padded = jnp.pad(wavefield, ((0, 0), (1, 1), (1, 1)))
    row_count = wavefield.shape[1]
    col_count = wavefield.shape[2]
    real_part = jnp.zeros((row_count, col_count), jnp.float32)
    imag_part = jnp.zeros((row_count, col_count), jnp.float32)
    for tap_index in range(9):
        row_shift = tap_index // 3
        col_shift = tap_index % 3
        near_real = padded[0, row_shift:row_shift + row_count, col_shift:col_shift + col_count]
        near_imag = padded[1, row_shift:row_shift + row_count, col_shift:col_shift + col_count]
        coef_real = filters_now[:, 0, tap_index][velocity_class]
        coef_imag = factor * filters_now[:, 1, tap_index][velocity_class]
        real_part = real_part + coef_real * near_real - coef_imag * near_imag
        imag_part = imag_part + coef_real * near_imag + coef_imag * near_real
    return jnp.stack([real_part, imag_part])

def lag_pick():
    depths = jnp.arange(STEPS, dtype=jnp.int32)
    spacing = jnp.abs(depths[:, None] - depths[None, :])
    return (spacing[None] == depths[:, None, None]).astype(jnp.float32)

def forward(model_cube, point_spread, spread_index):
    reach = PSF_SIDE // 2
    padded = jnp.pad(model_cube, ((0, 0), (reach, reach), (reach, reach)))
    picker = lag_pick()

    def one_brick(number):
        brick_row = number // BRICKS_Y
        brick_col = number % BRICKS_Y
        window = lax.dynamic_slice(padded, (jnp.zeros((), jnp.int32), brick_row * ROWS, brick_col * BCOLS), (STEPS, ROWS + 2 * reach, BCOLS + 2 * reach))
        kernel = jnp.einsum('lde,lab->edab', picker, point_spread[spread_index[brick_row, brick_col]], precision=HIGHEST)
        return lax.conv_general_dilated(window[None], kernel, (1, 1), 'VALID', precision=HIGHEST)[0]
    bricks = lax.map(one_brick, jnp.arange(BRICKS_X * BRICKS_Y, dtype=jnp.int32))
    bricks = bricks.reshape(BRICKS_X, BRICKS_Y, STEPS, ROWS, BCOLS)
    return bricks.transpose(2, 0, 3, 1, 4).reshape(STEPS, NX, NY)

def reference(receiver_field, source_field, velocity_class, filters, point_spread, spread_index):

    def one_frequency(summed, inputs):
        receiver, source, filters_now = inputs
        image_terms = []
        for depth_step in range(STEPS):
            receiver = advance(receiver, velocity_class, filters_now, 1.0)
            source = advance(source, velocity_class, filters_now, -1.0)
            image_terms.append(receiver[0] * source[0] + receiver[1] * source[1])
        return (summed + jnp.stack(image_terms, axis=1), None)
    start = jnp.zeros((NX, STEPS, NY), jnp.float32)
    summed, unused = lax.scan(one_frequency, start, (jnp.moveaxis(receiver_field, 1, 0), jnp.moveaxis(source_field, 1, 0), filters))
    migrated = summed * (1.0 / math.sqrt(NF))

    def operator(values):
        return forward(values, point_spread, spread_index)
    cell_count = STEPS * NX * NY
    residual = -jnp.transpose(migrated, (1, 0, 2))
    reflectivity = jnp.zeros_like(residual)
    energy = jnp.sum(residual * residual)
    for pass_index in range(PASSES):
        weight = 1.0 / jnp.sqrt(residual * residual + energy / cell_count)
        unused_out, pullback = jax.vjp(operator, reflectivity)
        descent = pullback(weight * residual)[0]
        image_of = operator(descent)
        step_length = jnp.sum(descent * descent) / jnp.sum(weight * image_of * image_of)
        reflectivity = reflectivity - step_length * descent
        residual = residual - step_length * image_of
        energy = jnp.sum(residual * residual)
    return (migrated, jnp.transpose(reflectivity, (1, 0, 2)), energy / cell_count)
```

```python
import functools
import math

import jax
import jax.numpy as jnp
from jax import lax
from jax.experimental import pallas as pl
from jax.experimental.pallas import tpu as pltpu
from jax.sharding import Mesh, PartitionSpec as P

STEPS = 2
SIDE = 15
REACH = 7
TAPS = SIDE * 16
LANES = 128
SHAPE = (8, 2, 4, 4, 2)
NAMES = ("z", "yh", "x", "yl", "c")
FREQ = ("z", "yh")
STRIP = ("x", "yl", "c")
NEAR = ("yh", "yl", "c")
FAR = ("z", "x")
GROUP = 8
CELLS = 1048576.0
ENERGY_LANE = 48

F32 = jnp.float32


def params():
    return pltpu.CompilerParams(vmem_limit_bytes=40 * 1024 * 1024)


def whole(count):
    return [pl.BlockSpec(memory_space=pltpu.VMEM)] * count


SMEM = pl.BlockSpec(memory_space=pltpu.SMEM)


def lane_iota():
    return lax.broadcasted_iota(jnp.int32, (8, LANES), 1)


def row_iota():
    return lax.broadcasted_iota(jnp.int32, (8, LANES), 0)


def pack_kernel(chunks, rec, src, cls, up, down):
    for k in range(chunks):
        at = slice(k * LANES, (k + 1) * LANES)
        for p, (field, part) in enumerate(((rec, 0), (rec, 1), (src, 0), (src, 1))):
            up[k, 2 * p : 2 * p + 2, :] = field[part, 0, 6:8, at]
            down[k, 2 * p : 2 * p + 2, :] = field[part, 0, 0:2, at]
        block, row = chunks + k // 8, k % 8
        up[block, row : row + 1, :] = cls[7:8, at].astype(F32)
        down[block, row : row + 1, :] = cls[0:1, at].astype(F32)


def pick(table, index):
    return jnp.take_along_axis(table, index, axis=1)


def image_kernel(
    chunks, place, rec, src, cls, filt, up, down, above, below, out, ext, left, right, coef, rim, img
):
    lane = lane_iota()
    row = row_iota()
    even = (row & 1) == 0
    zero = jnp.zeros((8, LANES), F32)
    first = place[0] == 0
    last = place[0] == place[2] - 1

    def tap(t):
        return jnp.broadcast_to(filt[t : t + 1, :], (8, LANES))

    for p in range(4):
        for side in (ext, left, right):
            for edge in (0, chunks + 1):
                for part in range(3):
                    side[p, edge, 8 * part : 8 * part + 8, :] = zero

    for m in range(3):
        rim[m, 0] = zero
        rim[m, chunks + 1] = zero

    def load(k, carry):
        at = pl.ds(pl.multiple_of(k * LANES, LANES), LANES)
        for p, (field, part) in enumerate(((rec, 0), (rec, 1), (src, 0), (src, 1))):
            ext[p, k + 1, 8:16, :] = field[part, 0, :, at]
            ext[p, k + 1, 0:8, :] = pltpu.roll(above[k], (6 - 2 * p) % 8, 0)
            ext[p, k + 1, 16:24, :] = pltpu.roll(below[k], (8 - 2 * p) % 8, 0)
        rim[0, k + 1] = jnp.where(even, above[k], up[k])
        rim[1, k + 1] = jnp.where(
            even, pltpu.roll(above[k], 7, 0), pltpu.roll(below[k], 1, 0)
        )
        rim[2, k + 1] = jnp.where(even, down[k], below[k])
        index = cls[:, at]
        for t in range(18):
            coef[t, k] = pick(tap(t), index)
        return carry

    lax.fori_loop(0, chunks, load, 0)

    def shift(value, before, after):
        to_right = jnp.where(lane == 0, pltpu.roll(before, 1, 1), pltpu.roll(value, 1, 1))
        to_left = jnp.where(lane == 127, pltpu.roll(after, 127, 1), pltpu.roll(value, 127, 1))
        return to_right, to_left

    def spread(k, carry):
        for p in range(4):
            for part in range(3):
                at = slice(8 * part, 8 * part + 8)
                a, b = shift(ext[p, k + 1, at, :], ext[p, k, at, :], ext[p, k + 2, at, :])
                left[p, k + 1, at, :] = a
                right[p, k + 1, at, :] = b
        return carry

    def own(k):
        parts = [None] * 4
        for t in range(9):
            plane = (left, ext, right)[t % 3]
            at = slice(7 + t // 3, 15 + t // 3)
            cr, ci = coef[t, k], coef[9 + t, k]
            rr, ri, sr, si = (plane[p, k + 1, at, :] for p in range(4))
            terms = (
                cr * rr - ci * ri,
                cr * ri + ci * rr,
                cr * sr + ci * si,
                cr * si - ci * sr,
            )
            parts = [v if q is None else q + v for q, v in zip(parts, terms)]
        return parts

    lax.fori_loop(0, chunks, spread, 0)

    def outside(k, carry):
        block = chunks + k // 8
        over = above[block, pl.ds(k % 8, 1), :]
        under = below[block, pl.ds(k % 8, 1), :]
        index = jnp.where(even, over, under).astype(jnp.int32)
        flip = jnp.where((row < 2) | (row >= 6), -1.0, 1.0)
        pair = (row & 2) == 0
        total = None
        for m in range(3):
            mid = rim[m, k + 1]
            a, b = shift(mid, rim[m, k], rim[m, k + 2])
            for n, v in enumerate((a, mid, b)):
                t = 3 * m + n
                swapped = flip * jnp.where(pair, pltpu.roll(v, 6, 0), pltpu.roll(v, 2, 0))
                term = pick(tap(t), index) * v + pick(tap(9 + t), index) * swapped
                total = term if total is None else total + term
        keep = jnp.where(even, jnp.where(first, 0.0, 1.0), jnp.where(last, 0.0, 1.0)) > 0.5
        rim[3, k + 1] = jnp.where(keep, total, 0.0)
        return carry

    lax.fori_loop(0, chunks, outside, 0)

    def step_one(k, carry):
        rr, ri, sr, si = own(k)
        img[0, k + 1] = sr * rr + si * ri
        for p, v in enumerate((rr, ri, sr, si)):
            rim[4 + p, k + 1] = v
        return carry

    lax.fori_loop(0, chunks, step_one, 0)

    def reload(k, carry):
        rows = rim[3, k + 1]
        for p in range(4):
            ext[p, k + 1, 8:16, :] = rim[4 + p, k + 1]
            ext[p, k + 1, 0:8, :] = pltpu.roll(rows, (7 - 2 * p) % 8, 0)
            ext[p, k + 1, 16:24, :] = pltpu.roll(rows, (7 - 2 * p) % 8, 0)
        return carry

    lax.fori_loop(0, chunks, reload, 0)
    lax.fori_loop(0, chunks, spread, 0)

    def step_two(k, carry):
        rr, ri, sr, si = own(k)
        img[1, k + 1] = sr * rr + si * ri
        return carry

    lax.fori_loop(0, chunks, step_two, 0)
    for d in range(STEPS):
        img[d, 0] = zero
        img[d, chunks + 1] = zero

    def give(k, carry):
        for d in range(STEPS):
            out[k, d, :, 0:LANES] = img[d, k + 1]
            out[k, d, :, LANES : 2 * LANES] = jnp.where(lane < 64, img[d, k + 2], img[d, k])
        return carry

    lax.fori_loop(0, chunks, give, 0)


def total_of(value):
    return jnp.sum(jnp.sum(value, axis=1, keepdims=True), axis=0, keepdims=True)


def sum_kernel(scaling, terms, migrated, payload):
    lane = lane_iota()
    energy = None
    halves = []
    for d in range(STEPS):
        pair = []
        for g in range(2):
            at = slice(g * LANES, (g + 1) * LANES)
            value = terms[0, d, :, at]
            for f in range(1, terms.shape[0]):
                value = value + terms[f, d, :, at]
            pair.append(value * scaling)
        migrated[:, d, :] = pair[0]
        term = pair[0] * pair[0]
        energy = term if energy is None else energy + term
        halves.append(pair)
    energy = total_of(energy)
    here = (lane >= 40) & (lane < 56)
    for d in range(STEPS):
        own = -halves[d][0]
        halo = jnp.where(here, energy, -halves[d][1])
        for n in range(payload.shape[0]):
            payload[n, d, :, 0:LANES] = own
            payload[n, d, :, LANES : 2 * LANES] = halo


def relay_kernel(place, near, energy, beside):
    total = near[0, 0, 0:1, LANES : 2 * LANES]
    for n in range(1, near.shape[0]):
        total = total + near[n, 0, 0:1, LANES : 2 * LANES]
    for n in range(energy.shape[0]):
        energy[n] = total
    start = place[3] * GROUP + jnp.where(place[4] < 4, 4, 0)
    for n in range(4):
        beside[n] = near[start + n]


def shifted(own, halo, by):
    lane = lax.broadcasted_iota(jnp.int32, own.shape, 1)
    if by == 0:
        return own, halo
    o, h = pltpu.roll(own, (-by) % LANES, 1), pltpu.roll(halo, (-by) % LANES, 1)
    near = lane < LANES - by if by > 0 else lane >= -by
    return jnp.where(near, o, h), jnp.where(near, h, o)


def table_kernel(place, index, spread, adjoint, forward):
    lane = lax.broadcasted_iota(jnp.int32, (16, LANES), 1)
    kind = lax.broadcasted_iota(jnp.int32, (16, LANES), 0)
    strips, groups = place[2], place[5]
    col = place[1]
    col_right = jnp.minimum(col + 1, groups - 1)
    col_left = jnp.maximum(col - 1, 0)
    for s in range(9):
        at = jnp.clip(place[0] + s - 4, 0, strips - 1)
        own = jnp.where(kind == index[at, col], 1.0, 0.0)
        halo = jnp.where(
            kind == jnp.where(lane < 64, index[at, col_right], index[at, col_left]), 1.0, 0.0
        )
        for sign in range(2):
            points = spread[sign]
            co = jnp.dot(points, own, precision=lax.Precision.HIGHEST, preferred_element_type=F32)
            ch = jnp.dot(points, halo, precision=lax.Precision.HIGHEST, preferred_element_type=F32)
            if 2 <= s < 7:
                forward[s - 2, 2 * sign] = co
                forward[s - 2, 2 * sign + 1] = ch
            for b in range(SIDE):
                rows = slice(16 * b, 16 * b + 16)
                so, sh = shifted(co[rows], ch[rows], REACH - b)
                adjoint[s, 2 * sign, rows, :] = so
                adjoint[s, 2 * sign + 1, rows, :] = sh


def operator_pass(count, place, resid, damping, adjoint, forward, rolled, acc, rolled_two, image):
    lane = lane_iota()
    row = row_iota()
    zero = jnp.zeros((8, LANES), F32)
    middle = count // 2

    for s in range(count):
        pairs = []
        for g in range(2):
            at = slice(g * LANES, (g + 1) * LANES)
            r0, r1 = resid[s, 0, :, at], resid[s, 1, :, at]
            u0 = r0 * (1.0 / jnp.sqrt(r0 * r0 + damping))
            u1 = r1 * (1.0 / jnp.sqrt(r1 * r1 + damping))
            pairs.append((u0 + u1, u0 - u1))
        for sign in range(2):
            for b in range(SIDE):
                o, h = shifted(pairs[0][sign], pairs[1][sign], REACH - b)
                rolled[b, 2 * sign, 8 * s : 8 * s + 8, :] = o
                rolled[b, 2 * sign + 1, 8 * s : 8 * s + 8, :] = h
    for q in range(4):
        for s in range(count + 2):
            acc[q, 8 * s : 8 * s + 8, :] = zero

    def back(s, carry):
        base = pl.multiple_of(8 * s, 8)
        for q in range(4):
            sums = [None] * SIDE
            for b in range(SIDE):
                value = rolled[b, q, pl.ds(base, 8), :]
                for a in range(SIDE):
                    r = 16 * b + a
                    term = adjoint[s, q, r : r + 1, :] * value
                    sums[a] = term if sums[a] is None else sums[a] + term
            lo, mid, hi = zero, sums[REACH], zero
            for a in range(SIDE):
                m = a - REACH
                if m == 0:
                    continue
                turned = pltpu.roll(sums[a], m % 8, 0)
                if m > 0:
                    mid = mid + jnp.where(row >= m, turned, 0.0)
                    hi = hi + jnp.where(row < m, turned, 0.0)
                else:
                    mid = mid + jnp.where(row < 8 + m, turned, 0.0)
                    lo = lo + jnp.where(row >= 8 + m, turned, 0.0)
            for n, v in enumerate((lo, mid, hi)):
                at = pl.ds(pl.multiple_of(base + 8 * n, 8), 8)
                acc[q, at, :] = acc[q, at, :] + v
        return carry

    lax.fori_loop(0, count, back, 0)

    col_ok = jnp.where(lane < 64, place[1] + 1, place[5] - place[1])
    halo_ok = col_ok < place[5]
    descent = []
    for s in range(1, count - 1):
        at = place[0] + s - middle
        row_ok = jnp.where((at >= 0) & (at < place[2]), 1.0, 0.0)
        for sign in range(2):
            o = acc[2 * sign, 8 * s + 8 : 8 * s + 16, :] * row_ok
            h = jnp.where(halo_ok, acc[2 * sign + 1, 8 * s + 8 : 8 * s + 16, :] * row_ok, 0.0)
            if s == middle:
                descent.append(o)
            for b in range(SIDE):
                so, sh = shifted(o, h, b - REACH)
                rolled_two[b, 2 * sign, 8 * s - 8 : 8 * s, :] = so
                rolled_two[b, 2 * sign + 1, 8 * s - 8 : 8 * s, :] = sh

    offset = 0 if count == 9 else 2

    def ahead(t, carry):
        base = pl.multiple_of(8 * t, 8)
        sums = [[None, None] for q in range(4)]
        for a in range(SIDE):
            for b in range(SIDE):
                r = 16 * b + a
                for q in range(4):
                    term = forward[t + offset, q, r : r + 1, :] * rolled_two[b, q, pl.ds(base + (a + 1), 8), :]
                    n = b % 2
                    sums[q][n] = term if sums[q][n] is None else sums[q][n] + term
        at = place[0] + t - (count - 4) // 2
        row_ok = jnp.where((at >= 0) & (at < place[2]), 0.5, 0.0)
        for g in range(2):
            plus = sums[g][0] + sums[g][1]
            minus = sums[2 + g][0] + sums[2 + g][1]
            q0, q1 = (plus + minus) * row_ok, (plus - minus) * row_ok
            if g == 1:
                q0, q1 = jnp.where(halo_ok, q0, 0.0), jnp.where(halo_ok, q1, 0.0)
            image[t, 0, :, g * LANES : (g + 1) * LANES] = q0
            image[t, 1, :, g * LANES : (g + 1) * LANES] = q1
        return carry

    lax.fori_loop(0, count - 4, ahead, 0)
    plus, minus = descent
    return 0.5 * (plus + minus), 0.5 * (plus - minus)


def five_sums(descent, resid, image, middle, damping, payload):
    lane = lax.broadcasted_iota(jnp.int32, (1, LANES), 1)
    sums = [jnp.zeros((8, LANES), F32)] * 5
    for d in range(STEPS):
        g, r, q = descent[d], resid[middle, d, :, 0:LANES], image[middle - 2, d, :, 0:LANES]
        w = 1.0 / jnp.sqrt(r * r + damping)
        for n, v in enumerate((g * g, w * q * q, r * q, q * q, r * r)):
            sums[n] = sums[n] + v
    value = jnp.zeros((1, LANES), F32)
    for n in range(5):
        value = jnp.where((lane >= 16 * n) & (lane < 16 * n + 16), total_of(sums[n]), value)
    for n in range(payload.shape[0]):
        payload[n] = value


def gathered(parts):
    total = parts[0]
    for n in range(1, parts.shape[0]):
        total = total + parts[n]
    return total


def at_lane(total, spot):
    lane = lax.broadcasted_iota(jnp.int32, (1, LANES), 1)
    return jnp.sum(jnp.where(lane == spot, total, 0.0), axis=1, keepdims=True)


def first_kernel(
    place, energies, near, beside, adjoint, forward, payload, resid, image, descent, energy,
    strips, rolled, acc, rolled_two,
):
    total = at_lane(gathered(energies), ENERGY_LANE)
    energy[...] = jnp.broadcast_to(total, (1, LANES))
    damping = total / CELLS
    low = jnp.where(place[4] < 4, 0, GROUP)
    base = jnp.where(place[4] < 4, 4, 0)
    for n in range(4):
        strips[low + n] = beside[n]
    for n in range(GROUP):
        strips[base + n] = near[place[3] * GROUP + n]
    start = lax.rem(place[4], 4)
    for s in range(9):
        resid[s] = strips[start + s]
    pair = operator_pass(9, place, resid, damping, adjoint, forward, rolled, acc, rolled_two, image)
    for d in range(STEPS):
        descent[d] = pair[d]
    five_sums(pair, resid, image, 4, damping, payload)


def step_and_energy(parts, energy):
    total = gathered(parts)
    square, curve, cross, image, before = (at_lane(total, 16 * n) for n in range(5))
    step = square / curve
    start = before if energy is None else energy
    after = start - 2.0 * step * cross + step * step * image
    return step, jnp.maximum(after, 0.0)


def second_kernel(
    place, parts, energy, resid_in, image_in, descent_in, adjoint, forward, payload, descent, model,
    resid, image, rolled, acc, rolled_two,
):
    step, after = step_and_energy(parts, energy[:, 0:1])
    damping = after / CELLS
    for s in range(5):
        for d in range(STEPS):
            resid[s, d] = resid_in[s + 2, d] - step * image_in[s, d]
    for d in range(STEPS):
        model[d] = -(step * descent_in[d])
    pair = operator_pass(
        5, place, resid, damping, adjoint.at[2:7], forward, rolled, acc, rolled_two, image
    )
    for d in range(STEPS):
        descent[d] = pair[d]
    five_sums(pair, resid, image, 2, damping, payload)


def last_kernel(parts, descent, model, reflectivity, misfit):
    step, after = step_and_energy(parts, None)
    for d in range(STEPS):
        reflectivity[:, d, :] = model[d] - step * descent[d]
    misfit[...] = after / CELLS


def shape(*dims):
    return jax.ShapeDtypeStruct(dims, F32)


def all_sum(parts):
    near = lax.all_to_all(parts, NEAR, 0, 0)
    total = jnp.sum(near, axis=0)
    ways = SHAPE[0] * SHAPE[2]
    return lax.all_to_all(jnp.broadcast_to(total[None], (ways, 1, LANES)), FAR, 0, 0)


def local(receiver_field, source_field, velocity_class, filters, point_spread, spread_index):
    strips = SHAPE[2] * SHAPE[3] * SHAPE[4]
    groups = SHAPE[0] * SHAPE[1]
    columns = velocity_class.shape[1]
    chunks = columns // LANES
    scaling = 1.0 / math.sqrt(groups)
    strip = lax.axis_index(STRIP)
    group = lax.axis_index(FREQ)
    half = lax.axis_index("yh")
    place = jnp.stack(
        [strip, group, jnp.int32(strips), half, lax.rem(strip, GROUP), jnp.int32(groups)]
    ).astype(jnp.int32)

    blocks = chunks + chunks // 8
    up, down = pl.pallas_call(
        functools.partial(pack_kernel, chunks),
        out_shape=(shape(blocks, 8, LANES), shape(blocks, 8, LANES)),
        in_specs=whole(3),
        out_specs=tuple(whole(2)),
        compiler_params=params(),
        name="pack",
    )(receiver_field, source_field, velocity_class)
    above = lax.ppermute(up, STRIP, [(i, i + 1) for i in range(strips - 1)])
    below = lax.ppermute(down, STRIP, [(i + 1, i) for i in range(strips - 1)])

    plus = point_spread[:, 0] + point_spread[:, 1]
    minus = point_spread[:, 0] - point_spread[:, 1]
    spread = jnp.stack([plus, minus]).transpose(0, 3, 2, 1)
    spread = jnp.pad(spread, ((0, 0), (0, 0), (0, 1), (0, 0))).reshape(2, TAPS, -1)
    adjoint, forward = pl.pallas_call(
        table_kernel,
        out_shape=(shape(9, 4, TAPS, LANES), shape(5, 4, TAPS, LANES)),
        in_specs=[SMEM, SMEM] + whole(1),
        out_specs=tuple(whole(2)),
        compiler_params=params(),
        cost_estimate=pl.CostEstimate(flops=100000000, bytes_accessed=8000000, transcendentals=0),
        name="tables",
    )(place, spread_index, spread)

    filt = filters[0].transpose(1, 2, 0).reshape(18, -1)
    filt = jnp.pad(filt, ((0, 0), (0, LANES - filt.shape[1])))
    planes = chunks + 2
    terms = pl.pallas_call(
        functools.partial(image_kernel, chunks),
        out_shape=shape(chunks, STEPS, 8, 2 * LANES),
        in_specs=[SMEM] + whole(8),
        out_specs=whole(1)[0],
        scratch_shapes=[
            pltpu.VMEM((4, planes, 24, LANES), F32),
            pltpu.VMEM((4, planes, 24, LANES), F32),
            pltpu.VMEM((4, planes, 24, LANES), F32),
            pltpu.VMEM((18, chunks, 8, LANES), F32),
            pltpu.VMEM((8, planes, 8, LANES), F32),
            pltpu.VMEM((STEPS, planes, 8, LANES), F32),
        ],
        compiler_params=params(),
        name="image",
    )(place, receiver_field, source_field, velocity_class, filt, up, down, above, below)
    terms = lax.all_to_all(terms, FREQ, 0, 0)

    nearby = SHAPE[1] * SHAPE[3] * SHAPE[4]
    far = SHAPE[0] * SHAPE[2]
    migrated, payload = pl.pallas_call(
        functools.partial(sum_kernel, scaling),
        out_shape=(shape(8, STEPS, LANES), shape(nearby, STEPS, 8, 2 * LANES)),
        in_specs=whole(1),
        out_specs=tuple(whole(2)),
        compiler_params=params(),
        name="stack",
    )(terms)
    near = lax.all_to_all(payload, NEAR, 0, 0)
    energies, beside = pl.pallas_call(
        relay_kernel,
        out_shape=(shape(far, 1, LANES), shape(4, STEPS, 8, 2 * LANES)),
        in_specs=[SMEM] + whole(1),
        out_specs=tuple(whole(2)),
        compiler_params=params(),
        name="relay",
    )(place, near)
    pairs = []
    for i in range(strips):
        to = i + GROUP if i % GROUP < 4 else i - GROUP
        if 0 <= to < strips:
            pairs.append((i, to))
    beside = lax.ppermute(beside, STRIP, pairs)
    energies = lax.all_to_all(energies, FAR, 0, 0)

    def scratch(count):
        return [
            pltpu.VMEM((SIDE, 4, 8 * count, LANES), F32),
            pltpu.VMEM((4, 8 * count + 16, LANES), F32),
            pltpu.VMEM((SIDE, 4, 8 * count - 16, LANES), F32),
        ]

    parts, resid, image, descent, energy = pl.pallas_call(
        first_kernel,
        out_shape=(
            shape(nearby, 1, LANES),
            shape(9, STEPS, 8, 2 * LANES),
            shape(5, STEPS, 8, 2 * LANES),
            shape(STEPS, 8, LANES),
            shape(1, LANES),
        ),
        in_specs=[SMEM] + whole(5),
        out_specs=tuple(whole(5)),
        scratch_shapes=[pltpu.VMEM((12, STEPS, 8, 2 * LANES), F32)] + scratch(9),
        compiler_params=params(),
        name="pass_one",
    )(place, energies, near, beside, adjoint, forward)
    parts = all_sum(parts)
    parts, descent, model = pl.pallas_call(
        second_kernel,
        out_shape=(shape(nearby, 1, LANES), shape(STEPS, 8, LANES), shape(STEPS, 8, LANES)),
        in_specs=[SMEM] + whole(7),
        out_specs=tuple(whole(3)),
        scratch_shapes=[
            pltpu.VMEM((5, STEPS, 8, 2 * LANES), F32),
            pltpu.VMEM((1, STEPS, 8, 2 * LANES), F32),
        ]
        + scratch(5),
        compiler_params=params(),
        name="pass_two",
    )(place, parts, energy, resid, image, descent, adjoint, forward)
    parts = all_sum(parts)
    reflectivity, misfit = pl.pallas_call(
        last_kernel,
        out_shape=(shape(8, STEPS, LANES), shape(1, 1)),
        in_specs=whole(3),
        out_specs=tuple(whole(2)),
        compiler_params=params(),
        name="last",
    )(parts, descent, model)
    return migrated, reflectivity, misfit.reshape(())


def solution(mesh):
    fine = Mesh(mesh.devices.reshape(SHAPE), NAMES)
    return jax.shard_map(
        local,
        mesh=fine,
        in_specs=(
            P(None, FREQ, STRIP, None),
            P(None, FREQ, STRIP, None),
            P(STRIP, None),
            P(FREQ, None, None, None),
            P(),
            P(),
        ),
        out_specs=(P(STRIP, None, FREQ), P(STRIP, None, FREQ), P()),
        check_vma=False,
    )
```

```python
import functools
import math

import jax
import jax.numpy as jnp
from jax import lax
from jax.experimental import pallas as pl
from jax.experimental.pallas import tpu as pltpu
from jax.sharding import Mesh, PartitionSpec as P

STEPS = 2
NCLASS = 8
SIDE = 15
REACH = 7
TAPS = SIDE * 16
LANES = 128
SHAPE = (8, 2, 4, 4, 2)
NAMES = ("z", "yh", "x", "yl", "c")
FREQ = ("z", "yh")
STRIP = ("x", "yl", "c")
NEAR = ("yh", "yl", "c")
FAR = ("z", "x")
GROUP = 8
CELLS = 1048576.0
ENERGY_LANE = 30

F32 = jnp.float32


def params(size=16):
    return pltpu.CompilerParams(vmem_limit_bytes=size * 1024 * 1024)


def whole(count):
    return [pl.BlockSpec(memory_space=pltpu.VMEM)] * count


SMEM = pl.BlockSpec(memory_space=pltpu.SMEM)
HBM = pl.BlockSpec(memory_space=pltpu.HBM)


def lane_iota():
    return lax.broadcasted_iota(jnp.int32, (8, LANES), 1)


def row_iota():
    return lax.broadcasted_iota(jnp.int32, (8, LANES), 0)


def each(count, step, by=4):
    def some(n, carry):
        for m in range(by):
            step(n * by + m)
        return carry

    lax.fori_loop(0, count // by, some, 0)


def fetch(pairs, sems):
    copies = [pltpu.make_async_copy(a, b, sems.at[n]) for n, (a, b) in enumerate(pairs)]
    for copy in copies:
        copy.start()
    for copy in copies:
        copy.wait()


def pack_kernel(
    chunks, rec_in, src_in, cls_in, up, down, field, kinds, rec, src, cls, sems
):
    fetch(((rec_in, rec), (src_in, src), (cls_in, cls)), sems)
    for k in range(chunks):
        at = slice(k * LANES, (k + 1) * LANES)
        for p, (plane, part) in enumerate(((rec, 0), (rec, 1), (src, 0), (src, 1))):
            value = plane[part, 0, :, at]
            field[p, k] = value
            up[k, 2 * p : 2 * p + 2, :] = value[6:8]
            down[k, 2 * p : 2 * p + 2, :] = value[0:2]
        block, row = chunks + k // 8, k % 8
        index = cls[:, at]
        kinds[k] = index
        up[block, row : row + 1, :] = index[7:8].astype(F32)
        down[block, row : row + 1, :] = index[0:1].astype(F32)


def pick(table, index):
    return jnp.take_along_axis(table, index, axis=1)


def tap_rows(filt, t):
    return jnp.broadcast_to(filt[t : t + 1, :], (8, LANES))


def neighbours(value, before, after):
    lane = lane_iota()
    to_right = jnp.where(lane == 0, pltpu.roll(before, 1, 1), pltpu.roll(value, 1, 1))
    to_left = jnp.where(lane == 127, pltpu.roll(after, 127, 1), pltpu.roll(value, 127, 1))
    return to_right, to_left


def inner_kernel(
    chunks, given, kinds, filters, one, two, edge, filt, field, ext, left, right, coef
):
    even = (row_iota() & 1) == 0
    zero = jnp.zeros((8, LANES), F32)
    same = lax.broadcasted_iota(jnp.int32, (9, 9), 0) == lax.broadcasted_iota(jnp.int32, (9, 9), 1)
    for part in range(2):
        filt[9 * part : 9 * part + 9, 0:NCLASS] = lax.dot_general(
            jnp.where(same, 1.0, 0.0),
            filters[0, :, part, :],
            (((1,), (1,)), ((), ())),
            precision=lax.Precision.HIGHEST,
            preferred_element_type=F32,
        )
    for p in range(4):
        for part in (0, chunks + 1):
            field[p, part] = zero

    def clear(k):
        for p in range(4):
            for side in (ext, left, right):
                side[p, k, 0:8, :] = zero
                side[p, k, 16:24, :] = zero

    each(chunks, clear)

    def load(k):
        for p in range(4):
            field[p, k + 1] = given[p, k]
        index = kinds[k]
        for t in range(18):
            coef[t, k] = pick(tap_rows(filt, t), index)
        rim = jnp.where(even, jnp.broadcast_to(index[0:1], (8, LANES)), jnp.broadcast_to(index[7:8], (8, LANES)))
        next_rim = jnp.where(even, jnp.broadcast_to(index[1:2], (8, LANES)), jnp.broadcast_to(index[6:7], (8, LANES)))
        for part in range(2):
            for n in range(3):
                t = 9 * part + n
                outward = jnp.where(even, tap_rows(filt, t), tap_rows(filt, t + 6))
                edge[3 * part + n, k] = pick(outward, rim)
                edge[6 + 3 * part + n, k] = pick(tap_rows(filt, t + 3), rim)
                edge[12 + 3 * part + n, k] = pick(outward, next_rim)

    each(chunks, load, 2)

    def spread(k):
        for p in range(4):
            value = field[p, k + 1]
            a, b = neighbours(value, field[p, k], field[p, k + 2])
            left[p, k, 8:16, :] = a
            ext[p, k, 8:16, :] = value
            right[p, k, 8:16, :] = b

    def step(out, keep, k):
        parts = [None] * 4
        for t in range(9):
            plane = (left, ext, right)[t % 3]
            at = slice(7 + t // 3, 15 + t // 3)
            cr, ci = coef[t, k], coef[9 + t, k]
            rr, ri, sr, si = (plane[p, k, at, :] for p in range(4))
            terms = (
                cr * rr - ci * ri,
                cr * ri + ci * rr,
                cr * sr + ci * si,
                cr * si - ci * sr,
            )
            parts = [v if q is None else q + v for q, v in zip(parts, terms)]
        for p in range(4):
            out[p, k] = parts[p]
            if keep:
                field[p, k + 1] = parts[p]

    each(chunks, spread)
    each(chunks, functools.partial(step, one, True), 2)
    each(chunks, spread)
    each(chunks, functools.partial(step, two, False), 2)


def edge_kernel(chunks, place, filt, one, two, edge, up, down, above, below, out, rim, img):
    lane = lane_iota()
    row = row_iota()
    even = (row & 1) == 0
    pair = (row & 2) == 0
    flip = jnp.where((row < 2) | (row >= 6), -1.0, 1.0)
    zero = jnp.zeros((8, LANES), F32)
    low = jnp.where(place[0] == 0, 0.0, 1.0)
    high = jnp.where(place[0] == place[2] - 1, 0.0, 1.0)
    keep = jnp.where(even, low, high)
    for m in range(5):
        rim[m, 0] = zero
        rim[m, chunks + 1] = zero

    def swap(v):
        return flip * jnp.where(pair, pltpu.roll(v, 6, 0), pltpu.roll(v, 2, 0))

    def near(m, k):
        mid = rim[m, k + 1]
        a, b = neighbours(mid, rim[m, k], rim[m, k + 2])
        return [(v, swap(v)) for v in (a, mid, b)]

    def load(k):
        rim[0, k + 1] = jnp.where(even, above[k], up[k])
        rim[1, k + 1] = jnp.where(even, pltpu.roll(above[k], 7, 0), pltpu.roll(below[k], 1, 0))
        rim[2, k + 1] = jnp.where(even, down[k], below[k])

    each(chunks, load)

    def first(k):
        block = chunks + k // 8
        over = above[block, pl.ds(k % 8, 1), :]
        under = below[block, pl.ds(k % 8, 1), :]
        index = jnp.where(even, over, under).astype(jnp.int32)
        total = zero
        change = zero
        for m in range(3):
            for n, (v, w) in enumerate(near(m, k)):
                t = 3 * m + n
                total = total + (pick(tap_rows(filt, t), index) * v + pick(tap_rows(filt, 9 + t), index) * w)
                if m == 1:
                    change = change + (edge[n, k] * v + edge[3 + n, k] * w)
        rim[3, k + 1] = total * keep
        rim[4, k + 1] = change

    each(chunks, first, 2)

    def second(k):
        rows, nexts = zero, zero
        for n, (v, w) in enumerate(near(3, k)):
            rows = rows + (edge[n, k] * v + edge[3 + n, k] * w)
        for n, (v, w) in enumerate(near(4, k)):
            rows = rows + (edge[6 + n, k] * v + edge[9 + n, k] * w)
            nexts = nexts + (edge[12 + n, k] * v + edge[15 + n, k] * w)
        change = rim[4, k + 1]
        turned = [[pltpu.roll(v, (first - 2 * m) % 8, 0) for m in range(4)] for v, first in ((change, 0), (rows, 0), (nexts, 1))]
        ones, twos = [], []
        for p in range(4):
            top, low_row = p, (p + 1) % 4
            ones.append(
                one[p, k]
                + jnp.where(row == 0, turned[0][top], jnp.where(row == 7, turned[0][low_row], 0.0))
            )
            outer = jnp.where(row == 0, turned[1][top], jnp.where(row == 7, turned[1][low_row], 0.0))
            inner = jnp.where(row == 1, turned[2][top], jnp.where(row == 6, turned[2][(p + 2) % 4], 0.0))
            twos.append(two[p, k] + (outer + inner))
        for d, (rr, ri, sr, si) in enumerate((ones, twos)):
            img[d, k + 1] = sr * rr + si * ri

    each(chunks, second, 2)
    for d in range(STEPS):
        img[d, 0] = zero
        img[d, chunks + 1] = zero

    outer = (lane < 32) | (lane >= 96)

    def give(k):
        sides = []
        for d in range(STEPS):
            out[k, d] = img[d, k + 1]
            sides.append(jnp.where(lane < 64, img[d, k + 2], img[d, k]))
        out[k, 2] = jnp.where(outer, sides[0], pltpu.roll(sides[1], 64, 1))

    each(chunks, give)


def total_of(value):
    return jnp.sum(jnp.sum(value, axis=1, keepdims=True), axis=0, keepdims=True)


def sum_kernel(scaling, terms, mark, migrated, payload):
    lane = lane_iota()
    values = []
    for d in range(3):
        value = terms[0, d]
        for f in range(1, terms.shape[0]):
            value = value + terms[f, d]
        values.append(value * scaling)
    for d in range(STEPS):
        migrated[:, d, :] = values[d]
    energy = total_of(values[0] * values[0] + values[1] * values[1])
    here = (lane >= 28) & (lane < 32)
    halo = jnp.where(here, energy, -values[2])
    for n in range(payload.shape[0]):
        payload[n, 0] = -values[0]
        payload[n, 1] = -values[1]
        payload[n, 2] = halo


def relay_kernel(place, near, energy, beside):
    total = near[0, 2, 0:1, :]
    for n in range(1, near.shape[0]):
        total = total + near[n, 2, 0:1, :]
    for n in range(energy.shape[0]):
        energy[n] = total
    start = place[3] * GROUP + jnp.where(place[4] < 4, 4, 0)
    for n in range(4):
        beside[n] = near[start + n]


def shifted(plus, minus, halo, by):
    if by == 0:
        return plus, minus, halo
    lane = lax.broadcasted_iota(jnp.int32, plus.shape, 1)
    turn, half = (-by) % LANES, (64 - by) % LANES
    p, m, h = (pltpu.roll(v, turn, 1) for v in (plus, minus, halo))
    m_half, h_half = pltpu.roll(minus, half, 1), pltpu.roll(halo, half, 1)
    if by > 0:
        ends, inner = lane >= LANES - by, (lane >= 64 - by) & (lane < 64)
    else:
        ends, inner = lane < -by, (lane >= 64) & (lane < 64 - by)
    return (
        jnp.where(ends, h, p),
        jnp.where(ends, h_half, m),
        jnp.where(ends, p, jnp.where(inner, m_half, h)),
    )


def halves(value):
    lane = lane_iota()
    turned = pltpu.roll(value, 64, 1)
    return jnp.where((lane < 32) | (lane >= 96), value + turned, turned - value)


def table_kernel(place, index, spread, tables_out, mark, tables, sems):
    kinds = spread.shape[1] // 2
    lane = lax.broadcasted_iota(jnp.int32, (2 * kinds, LANES), 1)
    kind = lax.broadcasted_iota(jnp.int32, (2 * kinds, LANES), 0)
    strips, groups = place[2], place[5]
    col = place[1]
    col_right = jnp.minimum(col + 1, groups - 1)
    col_left = jnp.maximum(col - 1, 0)
    points = spread[...]
    mark[...] = jnp.zeros((8, LANES), F32)
    copies = []

    def send(n):
        copy = pltpu.make_async_copy(tables.at[n], tables_out.at[n], sems.at[n])
        copy.start()
        copies.append(copy)

    for s in range(9):
        at = jnp.clip(place[0] + s - 4, 0, strips - 1)
        own = index[at, col]
        side = jnp.where((lane & 32) == 0, index[at, col_right], index[at, col_left])
        side = jnp.where((lane < 32) | (lane >= 96), side, side + kinds)
        chosen = [jnp.where(kind == v, 1.0, 0.0) for v in (own, own + kinds, side)]
        values = [
            jnp.dot(points, v, precision=lax.Precision.HIGHEST, preferred_element_type=F32)
            for v in chosen
        ]
        if 2 <= s < 7:
            for q in range(3):
                tables[7 + s, q] = values[q]
            send(7 + s)
        for b in range(SIDE):
            rows = slice(16 * b, 16 * b + 16)
            turned = shifted(*(v[rows] for v in values), REACH - b)
            for q in range(3):
                tables[s, q, rows, :] = turned[q]
        send(s)
    for copy in copies:
        copy.wait()


def table_copies(count, tables_in, tables, sems):
    skip, inner = (9 - count) // 2, 9 + (9 - count) // 2
    from_to = [(skip + n, n) for n in range(count)]
    from_to += [(inner + n, count + n) for n in range(count - 4)]
    for n, (a, b) in enumerate(from_to):
        pltpu.make_async_copy(tables_in.at[a], tables.at[b], sems.at[n]).start()

    def ready(n):
        pltpu.make_async_copy(tables_in.at[0], tables.at[n], sems.at[n]).wait()

    return ready


def operator_pass(count, place, resid, damping, tables, ready, rolled, acc, rolled_two, image):
    lane = lane_iota()
    row = row_iota()
    zero = jnp.zeros((8, LANES), F32)
    middle = count // 2

    for s in range(count):
        u0, u1, uh = (
            resid[s, n] * (1.0 / jnp.sqrt(resid[s, n] * resid[s, n] + damping)) for n in range(3)
        )
        base = (u0 + u1, u0 - u1, halves(uh))
        for b in range(SIDE):
            turned = shifted(*base, REACH - b)
            for q in range(3):
                rolled[b, q, 8 * s : 8 * s + 8, :] = turned[q]
    for q in range(3):
        for s in range(count + 2):
            acc[q, 8 * s : 8 * s + 8, :] = zero

    def back(s, carry):
        base = pl.multiple_of(8 * s, 8)
        ready(s)
        for q in range(3):
            sums = [None] * SIDE
            for b in range(SIDE):
                value = rolled[b, q, pl.ds(base, 8), :]
                for a in range(SIDE):
                    r = 16 * b + a
                    term = tables[s, q, r : r + 1, :] * value
                    sums[a] = term if sums[a] is None else sums[a] + term
            lo, mid, hi = zero, sums[REACH], zero
            for a in range(SIDE):
                m = a - REACH
                if m == 0:
                    continue
                turned = pltpu.roll(sums[a], m % 8, 0)
                if m > 0:
                    mid = mid + jnp.where(row >= m, turned, 0.0)
                    hi = hi + jnp.where(row < m, turned, 0.0)
                else:
                    mid = mid + jnp.where(row < 8 + m, turned, 0.0)
                    lo = lo + jnp.where(row >= 8 + m, turned, 0.0)
            for n, v in enumerate((lo, mid, hi)):
                at = pl.ds(pl.multiple_of(base + 8 * n, 8), 8)
                acc[q, at, :] = acc[q, at, :] + v
        return carry

    lax.fori_loop(0, count, back, 0)

    halo_ok = jnp.where((lane & 32) == 0, place[1] + 1, place[5] - place[1]) < place[5]
    descent = None
    for s in range(1, count - 1):
        at = place[0] + s - middle
        row_ok = jnp.where((at >= 0) & (at < place[2]), 1.0, 0.0)
        base = [acc[q, 8 * s + 8 : 8 * s + 16, :] * row_ok for q in range(3)]
        base[2] = jnp.where(halo_ok, base[2], 0.0)
        if s == middle:
            descent = base[:2]
        for b in range(SIDE):
            turned = shifted(*base, b - REACH)
            for q in range(3):
                rolled_two[b, q, 8 * s - 8 : 8 * s, :] = turned[q]

    def ahead(t, carry):
        base = pl.multiple_of(8 * t, 8)
        ready(count + t)
        sums = [[None, None] for q in range(3)]
        for a in range(SIDE):
            for b in range(SIDE):
                r = 16 * b + a
                for q in range(3):
                    term = tables[count + t, q, r : r + 1, :] * rolled_two[b, q, pl.ds(base + (a + 1), 8), :]
                    n = b % 2
                    sums[q][n] = term if sums[q][n] is None else sums[q][n] + term
        at = place[0] + t - (count - 4) // 2
        row_ok = jnp.where((at >= 0) & (at < place[2]), 0.5, 0.0)
        plus, minus, halo = ((v[0] + v[1]) * row_ok for v in sums)
        image[t, 0] = plus + minus
        image[t, 1] = plus - minus
        image[t, 2] = jnp.where(halo_ok, halves(halo), 0.0)
        return carry

    lax.fori_loop(0, count - 4, ahead, 0)
    plus, minus = descent
    return 0.5 * (plus + minus), 0.5 * (plus - minus)


def five_sums(descent, resid, image, middle, damping, payload):
    lane = lax.broadcasted_iota(jnp.int32, (1, LANES), 1)
    sums = [jnp.zeros((8, LANES), F32)] * 5
    for d in range(STEPS):
        g, r, q = descent[d], resid[middle, d], image[middle - 2, d]
        w = 1.0 / jnp.sqrt(r * r + damping)
        for n, v in enumerate((g * g, w * q * q, r * q, q * q, r * r)):
            sums[n] = sums[n] + v
    value = jnp.zeros((1, LANES), F32)
    for n in range(5):
        value = jnp.where((lane >= 16 * n) & (lane < 16 * n + 16), total_of(sums[n]), value)
    for n in range(payload.shape[0]):
        payload[n] = value


def gathered(parts):
    total = parts[0]
    for n in range(1, parts.shape[0]):
        total = total + parts[n]
    return total


def at_lane(total, spot):
    lane = lax.broadcasted_iota(jnp.int32, (1, LANES), 1)
    return jnp.sum(jnp.where(lane == spot, total, 0.0), axis=1, keepdims=True)


def first_kernel(
    place, energies, near, beside, tables_in, payload, state, descent, energy,
    strips, resid, image, tables, sems, rolled, acc, rolled_two,
):
    ready = table_copies(9, tables_in, tables, sems)
    total = at_lane(gathered(energies), ENERGY_LANE)
    energy[...] = jnp.broadcast_to(total, (1, LANES))
    damping = total / CELLS
    low = jnp.where(place[4] < 4, 0, GROUP)
    base = jnp.where(place[4] < 4, 4, 0)
    for n in range(4):
        strips[low + n] = beside[n]
    for n in range(GROUP):
        strips[base + n] = near[place[3] * GROUP + n]
    start = lax.rem(place[4], 4)
    for s in range(9):
        resid[s] = strips[start + s]
    pair = operator_pass(9, place, resid, damping, tables, ready, rolled, acc, rolled_two, image)
    for d in range(STEPS):
        descent[d] = pair[d]
    for s in range(5):
        state[s] = resid[s + 2]
        state[5 + s] = image[s]
    five_sums(pair, resid, image, 4, damping, payload)


def step_and_energy(parts, energy):
    total = gathered(parts)
    square, curve, cross, image, before = (at_lane(total, 16 * n) for n in range(5))
    step = square / curve
    start = before if energy is None else energy
    after = start - 2.0 * step * cross + step * step * image
    return step, jnp.maximum(after, 0.0)


def second_kernel(
    place, parts, energy, state, descent_in, tables_in, payload, descent, model,
    resid, image, tables, sems, rolled, acc, rolled_two,
):
    ready = table_copies(5, tables_in, tables, sems)
    step, after = step_and_energy(parts, energy[:, 0:1])
    damping = after / CELLS
    for s in range(5):
        for d in range(3):
            resid[s, d] = state[s, d] - step * state[5 + s, d]
    for d in range(STEPS):
        model[d] = -(step * descent_in[d])
    pair = operator_pass(5, place, resid, damping, tables, ready, rolled, acc, rolled_two, image)
    for d in range(STEPS):
        descent[d] = pair[d]
    five_sums(pair, resid, image, 2, damping, payload)


def last_kernel(parts, descent, model, reflectivity, misfit):
    step, after = step_and_energy(parts, None)
    for d in range(STEPS):
        reflectivity[:, d, :] = model[d] - step * descent[d]
    misfit[...] = after / CELLS


def shape(*dims):
    return jax.ShapeDtypeStruct(dims, F32)


def all_sum(parts):
    near = lax.all_to_all(parts, NEAR, 0, 0)
    total = jnp.sum(near, axis=0)
    ways = SHAPE[0] * SHAPE[2]
    return lax.all_to_all(jnp.broadcast_to(total[None], (ways, 1, LANES)), FAR, 0, 0)


def local(receiver_field, source_field, velocity_class, filters, point_spread, spread_index):
    strips = SHAPE[2] * SHAPE[3] * SHAPE[4]
    groups = SHAPE[0] * SHAPE[1]
    columns = velocity_class.shape[1]
    chunks = columns // LANES
    scaling = 1.0 / math.sqrt(groups)
    strip = lax.axis_index(STRIP)
    group = lax.axis_index(FREQ)
    half = lax.axis_index("yh")
    place = jnp.stack(
        [strip, group, jnp.int32(strips), half, lax.rem(strip, GROUP), jnp.int32(groups)]
    ).astype(jnp.int32)

    blocks = chunks + chunks // 8
    landing = [
        pltpu.VMEM(receiver_field.shape, F32),
        pltpu.VMEM(source_field.shape, F32),
        pltpu.VMEM(velocity_class.shape, jnp.int32),
    ]
    up, down, given, kinds = pl.pallas_call(
        functools.partial(pack_kernel, chunks),
        out_shape=(
            shape(blocks, 8, LANES),
            shape(blocks, 8, LANES),
            shape(4, chunks, 8, LANES),
            jax.ShapeDtypeStruct((chunks, 8, LANES), jnp.int32),
        ),
        in_specs=[HBM] * 3,
        out_specs=tuple(whole(4)),
        scratch_shapes=landing + [pltpu.SemaphoreType.DMA((3,))],
        compiler_params=params(16),
        name="pack",
    )(receiver_field, source_field, velocity_class)
    above = lax.ppermute(up, STRIP, [(i, i + 1) for i in range(strips - 1)])
    below = lax.ppermute(down, STRIP, [(i + 1, i) for i in range(strips - 1)])

    points = jnp.concatenate(
        [point_spread[:, 0] + point_spread[:, 1], point_spread[:, 0] - point_spread[:, 1]]
    ).transpose(2, 1, 0)
    points = jnp.pad(points, ((0, 0), (0, 1), (0, 0))).reshape(TAPS, -1)
    tables, mark = pl.pallas_call(
        table_kernel,
        out_shape=(shape(14, 3, TAPS, LANES), shape(8, LANES)),
        in_specs=[SMEM, SMEM] + whole(1),
        out_specs=(HBM, whole(1)[0]),
        scratch_shapes=[pltpu.VMEM((14, 3, TAPS, LANES), F32), pltpu.SemaphoreType.DMA((14,))],
        compiler_params=params(52),
        cost_estimate=pl.CostEstimate(flops=100000000, bytes_accessed=8000000, transcendentals=0),
        name="tables",
    )(place, spread_index, points)

    planes = chunks + 2
    one, two, edge, filt = pl.pallas_call(
        functools.partial(inner_kernel, chunks),
        out_shape=(
            shape(4, chunks, 8, LANES),
            shape(4, chunks, 8, LANES),
            shape(18, chunks, 8, LANES),
            shape(18, LANES),
        ),
        in_specs=whole(3),
        out_specs=tuple(whole(4)),
        scratch_shapes=[
            pltpu.VMEM((4, planes, 8, LANES), F32),
            pltpu.VMEM((4, chunks, 24, LANES), F32),
            pltpu.VMEM((4, chunks, 24, LANES), F32),
            pltpu.VMEM((4, chunks, 24, LANES), F32),
            pltpu.VMEM((18, chunks, 8, LANES), F32),
        ],
        compiler_params=params(),
        cost_estimate=pl.CostEstimate(flops=100000000, bytes_accessed=8000000, transcendentals=0),
        name="inner",
    )(given, kinds, filters)
    terms = pl.pallas_call(
        functools.partial(edge_kernel, chunks),
        out_shape=shape(chunks, 3, 8, LANES),
        in_specs=[SMEM] + whole(8),
        out_specs=whole(1)[0],
        scratch_shapes=[
            pltpu.VMEM((5, planes, 8, LANES), F32),
            pltpu.VMEM((STEPS, planes, 8, LANES), F32),
        ],
        compiler_params=params(),
        name="edges",
    )(place, filt, one, two, edge, up, down, above, below)
    terms = lax.all_to_all(terms, FREQ, 0, 0)

    nearby = SHAPE[1] * SHAPE[3] * SHAPE[4]
    far = SHAPE[0] * SHAPE[2]
    migrated, payload = pl.pallas_call(
        functools.partial(sum_kernel, scaling),
        out_shape=(shape(8, STEPS, LANES), shape(nearby, 3, 8, LANES)),
        in_specs=whole(2),
        out_specs=tuple(whole(2)),
        compiler_params=params(),
        name="stack",
    )(terms, mark)
    near = lax.all_to_all(payload, NEAR, 0, 0)
    energies, beside = pl.pallas_call(
        relay_kernel,
        out_shape=(shape(far, 1, LANES), shape(4, 3, 8, LANES)),
        in_specs=[SMEM] + whole(1),
        out_specs=tuple(whole(2)),
        compiler_params=params(),
        name="relay",
    )(place, near)
    pairs = []
    for i in range(strips):
        to = i + GROUP if i % GROUP < 4 else i - GROUP
        if 0 <= to < strips:
            pairs.append((i, to))
    beside = lax.ppermute(beside, STRIP, pairs)
    energies = lax.all_to_all(energies, FAR, 0, 0)

    def scratch(count):
        return [
            pltpu.VMEM((count, 3, 8, LANES), F32),
            pltpu.VMEM((count - 4, 3, 8, LANES), F32),
            pltpu.VMEM((2 * count - 4, 3, TAPS, LANES), F32),
            pltpu.SemaphoreType.DMA((2 * count - 4,)),
            pltpu.VMEM((SIDE, 3, 8 * count, LANES), F32),
            pltpu.VMEM((3, 8 * count + 16, LANES), F32),
            pltpu.VMEM((SIDE, 3, 8 * count - 16, LANES), F32),
        ]

    parts, state, descent, energy = pl.pallas_call(
        first_kernel,
        out_shape=(
            shape(nearby, 1, LANES),
            shape(10, 3, 8, LANES),
            shape(STEPS, 8, LANES),
            shape(1, LANES),
        ),
        in_specs=[SMEM] + whole(3) + [HBM],
        out_specs=tuple(whole(4)),
        scratch_shapes=[pltpu.VMEM((12, 3, 8, LANES), F32)] + scratch(9),
        compiler_params=params(52),
        name="pass_one",
    )(place, energies, near, beside, tables)
    parts = all_sum(parts)
    parts, descent, model = pl.pallas_call(
        second_kernel,
        out_shape=(shape(nearby, 1, LANES), shape(STEPS, 8, LANES), shape(STEPS, 8, LANES)),
        in_specs=[SMEM] + whole(4) + [HBM],
        out_specs=tuple(whole(3)),
        scratch_shapes=scratch(5),
        compiler_params=params(52),
        name="pass_two",
    )(place, parts, energy, state, descent, tables)
    parts = all_sum(parts)
    reflectivity, misfit = pl.pallas_call(
        last_kernel,
        out_shape=(shape(8, STEPS, LANES), shape(1, 1)),
        in_specs=whole(3),
        out_specs=tuple(whole(2)),
        compiler_params=params(),
        name="last",
    )(parts, descent, model)
    return migrated, reflectivity, misfit.reshape(())


def solution(mesh):
    fine = Mesh(mesh.devices.reshape(SHAPE), NAMES)
    return jax.shard_map(
        local,
        mesh=fine,
        in_specs=(
            P(None, FREQ, STRIP, None),
            P(None, FREQ, STRIP, None),
            P(STRIP, None),
            P(FREQ, None, None, None),
            P(),
            P(),
        ),
        out_specs=(P(STRIP, None, FREQ), P(STRIP, None, FREQ), P()),
        check_vma=False,
    )
```

```python
import functools
import math

import jax
import jax.numpy as jnp
from jax import lax
from jax.experimental import pallas as pl
from jax.experimental.pallas import tpu as pltpu
from jax.sharding import Mesh, PartitionSpec as P

STEPS = 2
NCLASS = 8
SIDE = 15
REACH = 7
TAPS = SIDE * 16
LANES = 128
SHAPE = (8, 2, 4, 4, 2)
NAMES = ("z", "yh", "x", "yl", "c")
FREQ = ("z", "yh")
STRIP = ("x", "yl", "c")
NEAR = ("yh", "yl", "c")
FAR = ("z", "x")
GROUP = 8
CELLS = 1048576.0
ENERGY_LANE = 30

F32 = jnp.float32


def params(size=16):
    return pltpu.CompilerParams(vmem_limit_bytes=size * 1024 * 1024)


def whole(count):
    return [pl.BlockSpec(memory_space=pltpu.VMEM)] * count


SMEM = pl.BlockSpec(memory_space=pltpu.SMEM)
HBM = pl.BlockSpec(memory_space=pltpu.HBM)


def lane_iota():
    return lax.broadcasted_iota(jnp.int32, (8, LANES), 1)


def row_iota():
    return lax.broadcasted_iota(jnp.int32, (8, LANES), 0)


def each(count, step):
    for k in range(count):
        step(k)


def fetch(pairs, sems):
    copies = [pltpu.make_async_copy(a, b, sems.at[n]) for n, (a, b) in enumerate(pairs)]
    for copy in copies:
        copy.start()
    for copy in copies:
        copy.wait()


def pack_kernel(
    chunks, rec_in, src_in, cls_in, inside, outside, field, kinds, rec, src, cls, sems
):
    fetch(((rec_in, rec), (src_in, src), (cls_in, cls)), sems)
    lower = jnp.full((8, LANES), lax.axis_index("c"), jnp.int32) == 0
    for k in range(chunks):
        at = slice(k * LANES, (k + 1) * LANES)
        for p, (plane, part) in enumerate(((rec, 0), (rec, 1), (src, 0), (src, 1))):
            value = plane[part, 0, :, at]
            field[p, k] = value
            inside[k, 2 * p : 2 * p + 2, :] = jnp.where(lower[0:2], value[6:8], value[0:2])
            outside[k, 2 * p : 2 * p + 2, :] = jnp.where(lower[0:2], value[0:2], value[6:8])
        block, row = chunks + k // 8, k % 8
        index = cls[:, at]
        kinds[k] = index
        top, bottom = index[0:1].astype(F32), index[7:8].astype(F32)
        inside[block, row : row + 1, :] = jnp.where(lower[0:1], bottom, top)
        outside[block, row : row + 1, :] = jnp.where(lower[0:1], top, bottom)


def pick(table, index):
    return jnp.take_along_axis(table, index, axis=1)


def tap_rows(filt, t):
    return jnp.broadcast_to(filt[t : t + 1, :], (8, LANES))


def neighbours(value, before, after):
    lane = lane_iota()
    to_right = jnp.where(lane == 0, pltpu.roll(before, 1, 1), pltpu.roll(value, 1, 1))
    to_left = jnp.where(lane == 127, pltpu.roll(after, 127, 1), pltpu.roll(value, 127, 1))
    return to_right, to_left


def inner_kernel(
    chunks, given, kinds, filters, one, two, edge, filt, field, ext, left, right, coef
):
    even = (row_iota() & 1) == 0
    zero = jnp.zeros((8, LANES), F32)
    same = lax.broadcasted_iota(jnp.int32, (9, 9), 0) == lax.broadcasted_iota(jnp.int32, (9, 9), 1)
    for part in range(2):
        filt[9 * part : 9 * part + 9, 0:NCLASS] = lax.dot_general(
            jnp.where(same, 1.0, 0.0),
            filters[0, :, part, :],
            (((1,), (1,)), ((), ())),
            precision=lax.Precision.HIGHEST,
            preferred_element_type=F32,
        )
    for p in range(4):
        for part in (0, chunks + 1):
            field[p, part] = zero

    def clear(k):
        for p in range(4):
            for side in (ext, left, right):
                side[p, k, 0:8, :] = zero
                side[p, k, 16:24, :] = zero

    each(chunks, clear)

    def load(k):
        for p in range(4):
            field[p, k + 1] = given[p, k]
        index = kinds[k]
        for t in range(18):
            coef[t, k] = pick(tap_rows(filt, t), index)
        rim = jnp.where(even, jnp.broadcast_to(index[0:1], (8, LANES)), jnp.broadcast_to(index[7:8], (8, LANES)))
        next_rim = jnp.where(even, jnp.broadcast_to(index[1:2], (8, LANES)), jnp.broadcast_to(index[6:7], (8, LANES)))
        for part in range(2):
            for n in range(3):
                t = 9 * part + n
                outward = jnp.where(even, tap_rows(filt, t), tap_rows(filt, t + 6))
                edge[3 * part + n, k] = pick(outward, rim)
                edge[6 + 3 * part + n, k] = pick(tap_rows(filt, t + 3), rim)
                edge[12 + 3 * part + n, k] = pick(outward, next_rim)

    each(chunks, load)

    def spread(k):
        for p in range(4):
            value = field[p, k + 1]
            a, b = neighbours(value, field[p, k], field[p, k + 2])
            left[p, k, 8:16, :] = a
            ext[p, k, 8:16, :] = value
            right[p, k, 8:16, :] = b

    def step(out, keep, k):
        parts = [None] * 4
        for t in range(9):
            plane = (left, ext, right)[t % 3]
            at = slice(7 + t // 3, 15 + t // 3)
            cr, ci = coef[t, k], coef[9 + t, k]
            rr, ri, sr, si = (plane[p, k, at, :] for p in range(4))
            terms = (
                cr * rr - ci * ri,
                cr * ri + ci * rr,
                cr * sr + ci * si,
                cr * si - ci * sr,
            )
            parts = [v if q is None else q + v for q, v in zip(parts, terms)]
        for p in range(4):
            out[p, k] = parts[p]
            if keep:
                field[p, k + 1] = parts[p]

    each(chunks, spread)
    each(chunks, functools.partial(step, one, True))
    each(chunks, spread)
    each(chunks, functools.partial(step, two, False))


def edge_kernel(
    chunks, place, filt, one, two, edge, inside, outside, partner, other, out, rim, img
):
    lane = lane_iota()
    row = row_iota()
    even = (row & 1) == 0
    pair = (row & 2) == 0
    flip = jnp.where((row < 2) | (row >= 6), -1.0, 1.0)
    zero = jnp.zeros((8, LANES), F32)
    lower = jnp.full((8, LANES), place[6], jnp.int32) == 0
    low = jnp.where(place[0] == 0, 0.0, 1.0)
    high = jnp.where(place[0] == place[2] - 1, 0.0, 1.0)
    keep = jnp.where(even, low, high)
    for m in range(5):
        rim[m, 0] = zero
        rim[m, chunks + 1] = zero

    def swap(v):
        return flip * jnp.where(pair, pltpu.roll(v, 6, 0), pltpu.roll(v, 2, 0))

    def near(m, k):
        mid = rim[m, k + 1]
        a, b = neighbours(mid, rim[m, k], rim[m, k + 2])
        return [(v, swap(v)) for v in (a, mid, b)]

    def load(k):
        up, down = jnp.where(lower, inside[k], outside[k]), jnp.where(lower, outside[k], inside[k])
        above, below = jnp.where(lower, other[k], partner[k]), jnp.where(lower, partner[k], other[k])
        rim[0, k + 1] = jnp.where(even, above, up)
        rim[1, k + 1] = jnp.where(even, pltpu.roll(above, 7, 0), pltpu.roll(below, 1, 0))
        rim[2, k + 1] = jnp.where(even, down, below)

    each(chunks, load)

    def first(k):
        block = chunks + k // 8
        near_rows = partner[block, k % 8 : k % 8 + 1, :]
        far_rows = other[block, k % 8 : k % 8 + 1, :]
        index = jnp.where(even == lower, far_rows, near_rows).astype(jnp.int32)
        total = zero
        change = zero
        for m in range(3):
            for n, (v, w) in enumerate(near(m, k)):
                t = 3 * m + n
                total = total + (pick(tap_rows(filt, t), index) * v + pick(tap_rows(filt, 9 + t), index) * w)
                if m == 1:
                    change = change + (edge[n, k] * v + edge[3 + n, k] * w)
        rim[3, k + 1] = total * keep
        rim[4, k + 1] = change

    each(chunks, first)

    def second(k):
        rows, nexts = zero, zero
        for n, (v, w) in enumerate(near(3, k)):
            rows = rows + (edge[n, k] * v + edge[3 + n, k] * w)
        for n, (v, w) in enumerate(near(4, k)):
            rows = rows + (edge[6 + n, k] * v + edge[9 + n, k] * w)
            nexts = nexts + (edge[12 + n, k] * v + edge[15 + n, k] * w)
        change = rim[4, k + 1]
        turned = [[pltpu.roll(v, (first - 2 * m) % 8, 0) for m in range(4)] for v, first in ((change, 0), (rows, 0), (nexts, 1))]
        ones, twos = [], []
        for p in range(4):
            top, low_row = p, (p + 1) % 4
            ones.append(
                one[p, k]
                + jnp.where(row == 0, turned[0][top], jnp.where(row == 7, turned[0][low_row], 0.0))
            )
            outer = jnp.where(row == 0, turned[1][top], jnp.where(row == 7, turned[1][low_row], 0.0))
            inner = jnp.where(row == 1, turned[2][top], jnp.where(row == 6, turned[2][(p + 2) % 4], 0.0))
            twos.append(two[p, k] + (outer + inner))
        for d, (rr, ri, sr, si) in enumerate((ones, twos)):
            img[d, k + 1] = sr * rr + si * ri

    each(chunks, second)
    for d in range(STEPS):
        img[d, 0] = zero
        img[d, chunks + 1] = zero

    outer = (lane < 32) | (lane >= 96)

    def give(k):
        sides = []
        for d in range(STEPS):
            out[k, d] = img[d, k + 1]
            sides.append(jnp.where(lane < 64, img[d, k + 2], img[d, k]))
        out[k, 2] = jnp.where(outer, sides[0], pltpu.roll(sides[1], 64, 1))

    each(chunks, give)


def total_of(value):
    return jnp.sum(jnp.sum(value, axis=1, keepdims=True), axis=0, keepdims=True)


def sum_kernel(scaling, terms, mark, migrated, payload):
    lane = lane_iota()
    values = []
    for d in range(3):
        value = terms[0, d]
        for f in range(1, terms.shape[0]):
            value = value + terms[f, d]
        values.append(value * scaling)
    for d in range(STEPS):
        migrated[:, d, :] = values[d]
    energy = total_of(values[0] * values[0] + values[1] * values[1])
    here = (lane >= 28) & (lane < 32)
    halo = jnp.where(here, energy, -values[2])
    for n in range(payload.shape[0]):
        payload[n, 0] = -values[0]
        payload[n, 1] = -values[1]
        payload[n, 2] = halo


def relay_kernel(place, near, energy, beside):
    total = near[0, 2]
    for n in range(1, near.shape[0]):
        total = total + near[n, 2]
    for n in range(energy.shape[0]):
        energy[n] = total[0 : energy.shape[1]]
    start = place[3] * GROUP + jnp.where(place[4] < 4, 4, 0)
    for n in range(4):
        beside[n] = near[start + n]


def shifted(plus, minus, halo, by):
    if by == 0:
        return plus, minus, halo
    lane = lax.broadcasted_iota(jnp.int32, plus.shape, 1)
    turn, half = (-by) % LANES, (64 - by) % LANES
    p, m, h = (pltpu.roll(v, turn, 1) for v in (plus, minus, halo))
    m_half, h_half = pltpu.roll(minus, half, 1), pltpu.roll(halo, half, 1)
    if by > 0:
        ends, inner = lane >= LANES - by, (lane >= 64 - by) & (lane < 64)
    else:
        ends, inner = lane < -by, (lane >= 64) & (lane < 64 - by)
    return (
        jnp.where(ends, h, p),
        jnp.where(ends, h_half, m),
        jnp.where(ends, p, jnp.where(inner, m_half, h)),
    )


def halves(value):
    lane = lane_iota()
    turned = pltpu.roll(value, 64, 1)
    return jnp.where((lane < 32) | (lane >= 96), value + turned, turned - value)


def strip_tables(place, index, points, s):
    kinds = points.shape[1] // 2
    lane = lax.broadcasted_iota(jnp.int32, (2 * kinds, LANES), 1)
    kind = lax.broadcasted_iota(jnp.int32, (2 * kinds, LANES), 0)
    strips, groups = place[2], place[5]
    col = place[1]
    col_right = jnp.minimum(col + 1, groups - 1)
    col_left = jnp.maximum(col - 1, 0)
    at = jnp.clip(place[0] + s - 4, 0, strips - 1)
    own = index[at, col]
    side = jnp.where((lane & 32) == 0, index[at, col_right], index[at, col_left])
    side = jnp.where((lane < 32) | (lane >= 96), side, side + kinds)
    chosen = [jnp.where(kind == v, 1.0, 0.0) for v in (own, own + kinds, side)]
    return [
        jnp.dot(points, v, precision=lax.Precision.HIGHEST, preferred_element_type=F32)
        for v in chosen
    ]


def adjoint_kernel(place, index, spread, tables_out, mark, tables, sems):
    points = spread[...]
    mark[...] = jnp.zeros((8, LANES), F32)
    copies = []

    def send(n):
        copy = pltpu.make_async_copy(tables.at[n], tables_out.at[n], sems.at[n])
        copy.start()
        copies.append(copy)

    for s in range(9):
        values = strip_tables(place, index, points, s)
        if s == 4:
            for q in range(3):
                tables[9, q] = values[q]
            send(9)
        for b in range(SIDE):
            rows = slice(16 * b, 16 * b + 16)
            turned = shifted(*(v[rows] for v in values), REACH - b)
            for q in range(3):
                tables[s, q, rows, :] = turned[q]
        send(s)
    for copy in copies:
        copy.wait()


def forward_kernel(place, index, spread, after, tables):
    points = spread[...]
    for s in range(5):
        values = strip_tables(place, index, points, s + 2)
        for q in range(3):
            tables[s, q] = values[q]


def table_copies(which, tables_in, tables, sems):
    for n, m in enumerate(which):
        pltpu.make_async_copy(tables_in.at[m], tables.at[n], sems.at[n]).start()

    def ready(n):
        pltpu.make_async_copy(tables_in.at[0], tables.at[n], sems.at[n]).wait()

    return ready


def operator_pass(
    count, place, resid, damping, tables, ready, forward, first_table, rolled, acc, rolled_two, image
):
    lane = lane_iota()
    row = row_iota()
    zero = jnp.zeros((8, LANES), F32)
    middle = count // 2

    for s in range(count):
        u0, u1, uh = (
            resid[s, n] * (1.0 / jnp.sqrt(resid[s, n] * resid[s, n] + damping)) for n in range(3)
        )
        base = (u0 + u1, u0 - u1, halves(uh))
        for b in range(SIDE):
            turned = shifted(*base, REACH - b)
            for q in range(3):
                rolled[b, q, 8 * s : 8 * s + 8, :] = turned[q]
    for q in range(3):
        for s in range(count + 2):
            acc[q, 8 * s : 8 * s + 8, :] = zero

    def back(taps, s):
        base = pl.multiple_of(8 * s, 8)
        ready(s)
        for q in range(3):
            sums = [None] * SIDE
            for b in range(SIDE):
                value = rolled[b, q, pl.ds(base, 8), :]
                for a in taps:
                    r = 16 * b + a
                    term = tables[s, q, r : r + 1, :] * value
                    sums[a] = term if sums[a] is None else sums[a] + term
            lo, mid, hi = zero, zero, zero
            for a in taps:
                m = a - REACH
                if m == 0:
                    mid = mid + sums[a]
                    continue
                turned = pltpu.roll(sums[a], m % 8, 0)
                if m > 0:
                    mid = mid + jnp.where(row >= m, turned, 0.0)
                    hi = hi + jnp.where(row < m, turned, 0.0)
                else:
                    mid = mid + jnp.where(row < 8 + m, turned, 0.0)
                    lo = lo + jnp.where(row >= 8 + m, turned, 0.0)
            for n, v in enumerate((lo, mid, hi)):
                at = pl.ds(pl.multiple_of(base + 8 * n, 8), 8)
                acc[q, at, :] = acc[q, at, :] + v

    for start, stop in ((0, 1), (1, count - 1), (count - 1, count)):
        taps = range(SIDE)
        if start == 0:
            taps = range(REACH + 1, SIDE)
        if stop == count:
            taps = range(REACH)

        def step(s, carry):
            back(taps, s)
            return carry

        lax.fori_loop(start, stop, step, 0)

    halo_ok = jnp.where((lane & 32) == 0, place[1] + 1, place[5] - place[1]) < place[5]
    descent = None
    for s in range(1, count - 1):
        at = place[0] + s - middle
        row_ok = jnp.where((at >= 0) & (at < place[2]), 1.0, 0.0)
        base = [acc[q, 8 * s + 8 : 8 * s + 16, :] * row_ok for q in range(3)]
        base[2] = jnp.where(halo_ok, base[2], 0.0)
        if s == middle:
            descent = base[:2]
        for b in range(SIDE):
            turned = shifted(*base, b - REACH)
            for q in range(3):
                rolled_two[b, q, 8 * s - 8 : 8 * s, :] = turned[q]

    def give(t, sums):
        at = place[0] + t - (count - 4) // 2
        row_ok = jnp.where((at >= 0) & (at < place[2]), 0.5, 0.0)
        plus, minus, halo = (v * row_ok for v in sums)
        image[t, 0] = plus + minus
        image[t, 1] = plus - minus
        image[t, 2] = jnp.where(halo_ok, halves(halo), 0.0)

    def taps_of(rows, base):
        for m in range(8):
            for b in range(SIDE):
                for q in range(3):
                    value = rolled_two[b, q, pl.ds(base + (m + 1), 8), :]
                    for t, low, sums in rows:
                        a = m if low else m + 8
                        if a < SIDE:
                            r = 16 * b + a
                            sums[q] = sums[q] + forward[first_table + t, q, r : r + 1, :] * value

    if first_table:
        ready(first_table)
    sums = [zero] * 3
    taps_of([(0, True, sums)], 0)

    def ahead(t, carry):
        old, new = list(carry), [zero] * 3
        taps_of([(t - 1, False, old), (t, True, new)], pl.multiple_of(8 * t, 8))
        give(t - 1, old)
        return tuple(new)

    sums = list(lax.fori_loop(1, count - 4, ahead, tuple(sums)))
    taps_of([(count - 5, False, sums)], 8 * (count - 4))
    give(count - 5, sums)
    plus, minus = descent
    return 0.5 * (plus + minus), 0.5 * (plus - minus)


def five_sums(descent, resid, image, middle, damping, payload):
    lane = lax.broadcasted_iota(jnp.int32, (1, LANES), 1)
    sums = [jnp.zeros((8, LANES), F32)] * 5
    for d in range(STEPS):
        g, r, q = descent[d], resid[middle, d], image[middle - 2, d]
        w = 1.0 / jnp.sqrt(r * r + damping)
        for n, v in enumerate((g * g, w * q * q, r * q, q * q, r * r)):
            sums[n] = sums[n] + v
    value = jnp.zeros((1, LANES), F32)
    for n in range(5):
        value = jnp.where((lane >= 16 * n) & (lane < 16 * n + 16), total_of(sums[n]), value)
    for n in range(payload.shape[0]):
        payload[n] = value


def gathered(parts):
    sums = [parts[n, 0:1] for n in range(4)]
    for n in range(4, parts.shape[0]):
        sums[n % 4] = sums[n % 4] + parts[n, 0:1]
    return (sums[0] + sums[1]) + (sums[2] + sums[3])


def at_lane(total, spot):
    lane = lax.broadcasted_iota(jnp.int32, (1, LANES), 1)
    return jnp.sum(jnp.where(lane == spot, total, 0.0), axis=1, keepdims=True)


def first_kernel(
    place, energies, near, beside, forward, tables_in, payload, state, descent, energy,
    strips, tables, sems, resid, image, rolled, acc, rolled_two,
):
    ready = table_copies(range(9), tables_in, tables, sems)
    total = at_lane(gathered(energies), ENERGY_LANE)
    energy[...] = jnp.broadcast_to(total, (1, LANES))
    damping = total / CELLS
    low = jnp.where(place[4] < 4, 0, GROUP)
    base = jnp.where(place[4] < 4, 4, 0)
    for n in range(4):
        strips[low + n] = beside[n]
    for n in range(GROUP):
        strips[base + n] = near[place[3] * GROUP + n]
    start = lax.rem(place[4], 4)
    for s in range(9):
        resid[s] = strips[start + s]
    pair = operator_pass(
        9, place, resid, damping, tables, ready, forward, 0, rolled, acc, rolled_two, image
    )
    for d in range(STEPS):
        descent[d] = pair[d]
    for s in range(5):
        state[s] = resid[s + 2]
        state[5 + s] = image[s]
    five_sums(pair, resid, image, 4, damping, payload)


def step_and_energy(parts, energy):
    total = gathered(parts)
    square, curve, cross, image, before = (at_lane(total, 16 * n) for n in range(5))
    step = square / curve
    start = before if energy is None else energy
    after = start - 2.0 * step * cross + step * step * image
    return step, jnp.maximum(after, 0.0)


def second_kernel(
    place, parts, energy, state, descent_in, tables_in, payload, descent, model,
    tables, sems, resid, image, rolled, acc, rolled_two,
):
    ready = table_copies((2, 3, 4, 5, 6, 9), tables_in, tables, sems)
    step, after = step_and_energy(parts, energy[:, 0:1])
    damping = after / CELLS
    for s in range(5):
        for d in range(3):
            resid[s, d] = state[s, d] - step * state[5 + s, d]
    for d in range(STEPS):
        model[d] = -(step * descent_in[d])

    pair = operator_pass(
        5, place, resid, damping, tables, ready, tables, 5, rolled, acc, rolled_two, image
    )
    for d in range(STEPS):
        descent[d] = pair[d]
    five_sums(pair, resid, image, 2, damping, payload)


def last_kernel(parts, descent, model, reflectivity, misfit):
    step, after = step_and_energy(parts, None)
    for d in range(STEPS):
        reflectivity[:, d, :] = model[d] - step * descent[d]
    misfit[...] = after / CELLS


def shape(*dims):
    return jax.ShapeDtypeStruct(dims, F32)


def all_sum(parts):
    near = lax.all_to_all(parts, NEAR, 0, 0)
    total = jnp.sum(near, axis=0)
    ways = SHAPE[0] * SHAPE[2]
    return lax.all_to_all(jnp.broadcast_to(total[None], (ways, 1, LANES)), FAR, 0, 0)


def local(receiver_field, source_field, velocity_class, filters, point_spread, spread_index):
    strips = SHAPE[2] * SHAPE[3] * SHAPE[4]
    groups = SHAPE[0] * SHAPE[1]
    columns = velocity_class.shape[1]
    chunks = columns // LANES
    scaling = 1.0 / math.sqrt(groups)
    strip = lax.axis_index(STRIP)
    group = lax.axis_index(FREQ)
    half = lax.axis_index("yh")
    place = jnp.stack(
        [strip, group, jnp.int32(strips), half, lax.rem(strip, GROUP), jnp.int32(groups), lax.axis_index("c")]
    ).astype(jnp.int32)

    blocks = chunks + chunks // 8
    landing = [
        pltpu.VMEM(receiver_field.shape, F32),
        pltpu.VMEM(source_field.shape, F32),
        pltpu.VMEM(velocity_class.shape, jnp.int32),
    ]
    inside, outside, given, kinds = pl.pallas_call(
        functools.partial(pack_kernel, chunks),
        out_shape=(
            shape(blocks, 8, LANES),
            shape(blocks, 8, LANES),
            shape(4, chunks, 8, LANES),
            jax.ShapeDtypeStruct((chunks, 8, LANES), jnp.int32),
        ),
        in_specs=[HBM] * 3,
        out_specs=tuple(whole(4)),
        scratch_shapes=landing + [pltpu.SemaphoreType.DMA((3,))],
        compiler_params=params(),
        name="pack",
    )(receiver_field, source_field, velocity_class)
    swaps = [(i, i ^ 1) for i in range(strips)]
    partner = lax.ppermute(inside, STRIP, swaps)
    crossings = [(i, i - 1 if i % 2 == 0 else i + 1) for i in range(1, strips - 1)]
    other = lax.ppermute(outside, STRIP, crossings)

    points = jnp.concatenate(
        [point_spread[:, 0] + point_spread[:, 1], point_spread[:, 0] - point_spread[:, 1]]
    ).transpose(2, 1, 0)
    points = jnp.pad(points, ((0, 0), (0, 1), (0, 0))).reshape(TAPS, -1)
    tables, mark = pl.pallas_call(
        adjoint_kernel,
        out_shape=(shape(24, 3, TAPS, LANES), shape(8, LANES)),
        in_specs=[SMEM, SMEM] + whole(1),
        out_specs=(HBM, whole(1)[0]),
        scratch_shapes=[pltpu.VMEM((10, 3, TAPS, LANES), F32), pltpu.SemaphoreType.DMA((10,))],
        compiler_params=params(47),
        cost_estimate=pl.CostEstimate(flops=100000000, bytes_accessed=8000000, transcendentals=0),
        name="tables",
    )(place, spread_index, points)

    planes = chunks + 2
    one, two, edge, filt = pl.pallas_call(
        functools.partial(inner_kernel, chunks),
        out_shape=(
            shape(4, chunks, 8, LANES),
            shape(4, chunks, 8, LANES),
            shape(18, chunks, 8, LANES),
            shape(18, LANES),
        ),
        in_specs=whole(3),
        out_specs=tuple(whole(4)),
        scratch_shapes=[
            pltpu.VMEM((4, planes, 8, LANES), F32),
            pltpu.VMEM((4, chunks, 24, LANES), F32),
            pltpu.VMEM((4, chunks, 24, LANES), F32),
            pltpu.VMEM((4, chunks, 24, LANES), F32),
            pltpu.VMEM((18, chunks, 8, LANES), F32),
        ],
        compiler_params=params(),
        cost_estimate=pl.CostEstimate(flops=100000000, bytes_accessed=8000000, transcendentals=0),
        name="inner",
    )(given, kinds, filters)
    terms = pl.pallas_call(
        functools.partial(edge_kernel, chunks),
        out_shape=shape(chunks, 3, 8, LANES),
        in_specs=[SMEM] + whole(8),
        out_specs=whole(1)[0],
        scratch_shapes=[
            pltpu.VMEM((5, planes, 8, LANES), F32),
            pltpu.VMEM((STEPS, planes, 8, LANES), F32),
        ],
        compiler_params=params(),
        name="edges",
    )(place, filt, one, two, edge, inside, outside, partner, other)
    terms = lax.all_to_all(terms, FREQ, 0, 0)

    nearby = SHAPE[1] * SHAPE[3] * SHAPE[4]
    far = SHAPE[0] * SHAPE[2]
    migrated, payload = pl.pallas_call(
        functools.partial(sum_kernel, scaling),
        out_shape=(shape(8, STEPS, LANES), shape(nearby, 3, 8, LANES)),
        in_specs=whole(2),
        out_specs=tuple(whole(2)),
        compiler_params=params(),
        name="stack",
    )(terms, mark)
    near = lax.all_to_all(payload, NEAR, 0, 0)
    energies, beside = pl.pallas_call(
        relay_kernel,
        out_shape=(shape(far, 2, LANES), shape(4, 3, 8, LANES)),
        in_specs=[SMEM] + whole(1),
        out_specs=tuple(whole(2)),
        compiler_params=params(),
        name="relay",
    )(place, near)
    exchanged = lax.all_to_all(energies, FAR, 0, 0)
    pairs = []
    for i in range(strips):
        to = i + GROUP if i % GROUP < 4 else i - GROUP
        if 0 <= to < strips:
            pairs.append((i, to))
    beside = lax.ppermute(beside, STRIP, pairs)
    forward = pl.pallas_call(
        forward_kernel,
        out_shape=shape(5, 3, TAPS, LANES),
        in_specs=[SMEM, SMEM] + whole(2),
        out_specs=whole(1)[0],
        compiler_params=params(),
        cost_estimate=pl.CostEstimate(flops=100000000, bytes_accessed=8000000, transcendentals=0),
        name="ahead",
    )(place, spread_index, points, energies)

    def scratch(count):
        return [
            pltpu.VMEM((count, 3, 8, LANES), F32),
            pltpu.VMEM((count - 4, 3, 8, LANES), F32),
            pltpu.VMEM((SIDE, 3, 8 * count, LANES), F32),
            pltpu.VMEM((3, 8 * count + 16, LANES), F32),
            pltpu.VMEM((SIDE, 3, 8 * count - 16, LANES), F32),
        ]

    parts, state, descent, energy = pl.pallas_call(
        first_kernel,
        out_shape=(
            shape(nearby, 1, LANES),
            shape(10, 3, 8, LANES),
            shape(STEPS, 8, LANES),
            shape(1, LANES),
        ),
        in_specs=[SMEM] + whole(4) + [HBM],
        out_specs=tuple(whole(4)),
        scratch_shapes=[
            pltpu.VMEM((12, 3, 8, LANES), F32),
            pltpu.VMEM((9, 3, TAPS, LANES), F32),
            pltpu.SemaphoreType.DMA((9,)),
        ]
        + scratch(9),
        compiler_params=params(47),
        name="pass_one",
    )(place, exchanged, near, beside, forward, tables)
    parts = all_sum(parts)
    parts, descent, model = pl.pallas_call(
        second_kernel,
        out_shape=(shape(nearby, 1, LANES), shape(STEPS, 8, LANES), shape(STEPS, 8, LANES)),
        in_specs=[SMEM] + whole(4) + [HBM],
        out_specs=tuple(whole(3)),
        scratch_shapes=[pltpu.VMEM((6, 3, TAPS, LANES), F32), pltpu.SemaphoreType.DMA((6,))]
        + scratch(5),
        compiler_params=params(47),
        name="pass_two",
    )(place, parts, energy, state, descent, tables)
    parts = all_sum(parts)
    reflectivity, misfit = pl.pallas_call(
        last_kernel,
        out_shape=(shape(8, STEPS, LANES), shape(1, 1)),
        in_specs=whole(3),
        out_specs=tuple(whole(2)),
        compiler_params=params(),
        name="last",
    )(parts, descent, model)
    return migrated, reflectivity, misfit.reshape(())


def solution(mesh):
    fine = Mesh(mesh.devices.reshape(SHAPE), NAMES)
    return jax.shard_map(
        local,
        mesh=fine,
        in_specs=(
            P(None, FREQ, STRIP, None),
            P(None, FREQ, STRIP, None),
            P(STRIP, None),
            P(FREQ, None, None, None),
            P(),
            P(),
        ),
        out_specs=(P(STRIP, None, FREQ), P(STRIP, None, FREQ), P()),
        check_vma=False,
    )
```

```python
import functools
import math

import jax
import jax.numpy as jnp
from jax import lax
from jax.experimental import pallas as pl
from jax.experimental.pallas import tpu as pltpu
from jax.sharding import Mesh, PartitionSpec as P

STEPS = 2
NCLASS = 8
SIDE = 15
REACH = 7
TAPS = SIDE * 16
LANES = 128
SHAPE = (8, 2, 4, 4, 2)
NAMES = ("z", "yh", "x", "yl", "c")
FREQ = ("z", "yh")
STRIP = ("x", "yl", "c")
NEAR = ("yh", "yl", "c")
FAR = ("z", "x")
GROUP = 8
CELLS = 1048576.0
ENERGY_LANE = 30

F32 = jnp.float32


def params(size=16):
    return pltpu.CompilerParams(vmem_limit_bytes=size * 1024 * 1024)


def whole(count):
    return [pl.BlockSpec(memory_space=pltpu.VMEM)] * count


SMEM = pl.BlockSpec(memory_space=pltpu.SMEM)
HBM = pl.BlockSpec(memory_space=pltpu.HBM)


def lane_iota():
    return lax.broadcasted_iota(jnp.int32, (8, LANES), 1)


def row_iota():
    return lax.broadcasted_iota(jnp.int32, (8, LANES), 0)


def whereabouts():
    z, yh, x, yl, c = (lax.axis_index(name) for name in NAMES)
    spot = yl * SHAPE[4] + c
    strips, groups = SHAPE[2] * SHAPE[3] * SHAPE[4], SHAPE[0] * SHAPE[1]
    return x * GROUP + spot, z * SHAPE[1] + yh, strips, yh, spot, groups, c


def each(count, step):
    for k in range(count):
        step(k)


def fetch(pairs, sems):
    copies = [pltpu.make_async_copy(a, b, sems.at[n]) for n, (a, b) in enumerate(pairs)]
    for copy in copies:
        copy.start()
    for copy in copies:
        copy.wait()


def pack_kernel(
    chunks, rec_in, src_in, cls_in, inside, outside, field, kinds, rec, src, cls, sems
):
    fetch(((rec_in, rec), (src_in, src), (cls_in, cls)), sems)
    lower = jnp.full((8, LANES), lax.axis_index("c"), jnp.int32) == 0
    for k in range(chunks):
        at = slice(k * LANES, (k + 1) * LANES)
        for p, (plane, part) in enumerate(((rec, 0), (rec, 1), (src, 0), (src, 1))):
            value = plane[part, 0, :, at]
            field[p, k] = value
            inside[k, 2 * p : 2 * p + 2, :] = jnp.where(lower[0:2], value[6:8], value[0:2])
            outside[k, 2 * p : 2 * p + 2, :] = jnp.where(lower[0:2], value[0:2], value[6:8])
        block, row = chunks + k // 8, k % 8
        index = cls[:, at]
        kinds[k] = index
        top, bottom = index[0:1].astype(F32), index[7:8].astype(F32)
        inside[block, row : row + 1, :] = jnp.where(lower[0:1], bottom, top)
        outside[block, row : row + 1, :] = jnp.where(lower[0:1], top, bottom)


def pick(table, index):
    return jnp.take_along_axis(table, index, axis=1)


def tap_rows(filt, t):
    return jnp.broadcast_to(filt[t : t + 1, :], (8, LANES))


def neighbours(value, before, after):
    lane = lane_iota()
    to_right = jnp.where(lane == 0, pltpu.roll(before, 1, 1), pltpu.roll(value, 1, 1))
    to_left = jnp.where(lane == 127, pltpu.roll(after, 127, 1), pltpu.roll(value, 127, 1))
    return to_right, to_left


def inner_kernel(
    chunks, given, kinds, filters, one, two, edge, filt, field, ext, left, right, coef
):
    even = (row_iota() & 1) == 0
    zero = jnp.zeros((8, LANES), F32)
    same = lax.broadcasted_iota(jnp.int32, (9, 9), 0) == lax.broadcasted_iota(jnp.int32, (9, 9), 1)
    for part in range(2):
        filt[9 * part : 9 * part + 9, 0:NCLASS] = lax.dot_general(
            jnp.where(same, 1.0, 0.0),
            filters[0, :, part, :],
            (((1,), (1,)), ((), ())),
            precision=lax.Precision.HIGHEST,
            preferred_element_type=F32,
        )
    for p in range(4):
        for part in (0, chunks + 1):
            field[p, part] = zero

    def clear(k):
        for p in range(4):
            for side in (ext, left, right):
                side[p, k, 0:8, :] = zero
                side[p, k, 16:24, :] = zero

    each(chunks, clear)

    def load(k):
        for p in range(4):
            field[p, k + 1] = given[p, k]
        index = kinds[k]
        for t in range(18):
            coef[t, k] = pick(tap_rows(filt, t), index)
        rim = jnp.where(even, jnp.broadcast_to(index[0:1], (8, LANES)), jnp.broadcast_to(index[7:8], (8, LANES)))
        next_rim = jnp.where(even, jnp.broadcast_to(index[1:2], (8, LANES)), jnp.broadcast_to(index[6:7], (8, LANES)))
        for part in range(2):
            for n in range(3):
                t = 9 * part + n
                outward = jnp.where(even, tap_rows(filt, t), tap_rows(filt, t + 6))
                edge[3 * part + n, k] = pick(outward, rim)
                edge[6 + 3 * part + n, k] = pick(tap_rows(filt, t + 3), rim)
                edge[12 + 3 * part + n, k] = pick(outward, next_rim)

    each(chunks, load)

    def spread(k):
        for p in range(4):
            value = field[p, k + 1]
            a, b = neighbours(value, field[p, k], field[p, k + 2])
            left[p, k, 8:16, :] = a
            ext[p, k, 8:16, :] = value
            right[p, k, 8:16, :] = b

    def step(out, keep, k):
        parts = [None] * 4
        for t in range(9):
            plane = (left, ext, right)[t % 3]
            at = slice(7 + t // 3, 15 + t // 3)
            cr, ci = coef[t, k], coef[9 + t, k]
            rr, ri, sr, si = (plane[p, k, at, :] for p in range(4))
            terms = (
                cr * rr - ci * ri,
                cr * ri + ci * rr,
                cr * sr + ci * si,
                cr * si - ci * sr,
            )
            parts = [v if q is None else q + v for q, v in zip(parts, terms)]
        for p in range(4):
            out[p, k] = parts[p]
            if keep:
                field[p, k + 1] = parts[p]

    each(chunks, spread)
    each(chunks, functools.partial(step, one, True))
    each(chunks, spread)
    each(chunks, functools.partial(step, two, False))


def edge_kernel(
    chunks, filt, one, two, edge, inside, outside, partner, other, out, rim, img
):
    place = whereabouts()
    lane = lane_iota()
    row = row_iota()
    even = (row & 1) == 0
    pair = (row & 2) == 0
    flip = jnp.where((row < 2) | (row >= 6), -1.0, 1.0)
    zero = jnp.zeros((8, LANES), F32)
    lower = jnp.full((8, LANES), place[6], jnp.int32) == 0
    low = jnp.where(place[0] == 0, 0.0, 1.0)
    high = jnp.where(place[0] == place[2] - 1, 0.0, 1.0)
    keep = jnp.where(even, low, high)
    for m in range(5):
        rim[m, 0] = zero
        rim[m, chunks + 1] = zero

    def swap(v):
        return flip * jnp.where(pair, pltpu.roll(v, 6, 0), pltpu.roll(v, 2, 0))

    def near(m, k):
        mid = rim[m, k + 1]
        a, b = neighbours(mid, rim[m, k], rim[m, k + 2])
        return [(v, swap(v)) for v in (a, mid, b)]

    def load(k):
        up, down = jnp.where(lower, inside[k], outside[k]), jnp.where(lower, outside[k], inside[k])
        above, below = jnp.where(lower, other[k], partner[k]), jnp.where(lower, partner[k], other[k])
        rim[0, k + 1] = jnp.where(even, above, up)
        rim[1, k + 1] = jnp.where(even, pltpu.roll(above, 7, 0), pltpu.roll(below, 1, 0))
        rim[2, k + 1] = jnp.where(even, down, below)

    each(chunks, load)

    def first(k):
        block = chunks + k // 8
        near_rows = partner[block, k % 8 : k % 8 + 1, :]
        far_rows = other[block, k % 8 : k % 8 + 1, :]
        index = jnp.where(even == lower, far_rows, near_rows).astype(jnp.int32)
        total = zero
        change = zero
        for m in range(3):
            for n, (v, w) in enumerate(near(m, k)):
                t = 3 * m + n
                total = total + (pick(tap_rows(filt, t), index) * v + pick(tap_rows(filt, 9 + t), index) * w)
                if m == 1:
                    change = change + (edge[n, k] * v + edge[3 + n, k] * w)
        rim[3, k + 1] = total * keep
        rim[4, k + 1] = change

    each(chunks, first)

    def second(k):
        rows, nexts = zero, zero
        for n, (v, w) in enumerate(near(3, k)):
            rows = rows + (edge[n, k] * v + edge[3 + n, k] * w)
        for n, (v, w) in enumerate(near(4, k)):
            rows = rows + (edge[6 + n, k] * v + edge[9 + n, k] * w)
            nexts = nexts + (edge[12 + n, k] * v + edge[15 + n, k] * w)
        change = rim[4, k + 1]
        turned = [[pltpu.roll(v, (first - 2 * m) % 8, 0) for m in range(4)] for v, first in ((change, 0), (rows, 0), (nexts, 1))]
        ones, twos = [], []
        for p in range(4):
            top, low_row = p, (p + 1) % 4
            ones.append(
                one[p, k]
                + jnp.where(row == 0, turned[0][top], jnp.where(row == 7, turned[0][low_row], 0.0))
            )
            outer = jnp.where(row == 0, turned[1][top], jnp.where(row == 7, turned[1][low_row], 0.0))
            inner = jnp.where(row == 1, turned[2][top], jnp.where(row == 6, turned[2][(p + 2) % 4], 0.0))
            twos.append(two[p, k] + (outer + inner))
        for d, (rr, ri, sr, si) in enumerate((ones, twos)):
            img[d, k + 1] = sr * rr + si * ri

    each(chunks, second)
    for d in range(STEPS):
        img[d, 0] = zero
        img[d, chunks + 1] = zero

    outer = (lane < 32) | (lane >= 96)

    def give(k):
        sides = []
        for d in range(STEPS):
            out[k, d] = img[d, k + 1]
            sides.append(jnp.where(lane < 64, img[d, k + 2], img[d, k]))
        out[k, 2] = jnp.where(outer, sides[0], pltpu.roll(sides[1], 64, 1))

    each(chunks, give)


def total_of(value):
    return jnp.sum(jnp.sum(value, axis=1, keepdims=True), axis=0, keepdims=True)


def sum_kernel(scaling, terms, mark, migrated, payload):
    lane = lane_iota()
    values = []
    for d in range(3):
        value = terms[0, d]
        for f in range(1, terms.shape[0]):
            value = value + terms[f, d]
        values.append(value * scaling)
    for d in range(STEPS):
        migrated[:, d, :] = values[d]
    energy = total_of(values[0] * values[0] + values[1] * values[1])
    here = (lane >= 28) & (lane < 32)
    halo = jnp.where(here, energy, -values[2])
    for n in range(payload.shape[0]):
        payload[n, 0] = -values[0]
        payload[n, 1] = -values[1]
        payload[n, 2] = halo


def relay_kernel(near, energy, beside):
    place = whereabouts()
    total = near[0, 2]
    for n in range(1, near.shape[0]):
        total = total + near[n, 2]
    for n in range(energy.shape[0]):
        energy[n] = total[0 : energy.shape[1]]
    start = place[3] * GROUP + jnp.where(place[4] < 4, 4, 0)
    for n in range(4):
        beside[n] = near[start + n]


def shifted(plus, minus, halo, by):
    if by == 0:
        return plus, minus, halo
    lane = lax.broadcasted_iota(jnp.int32, plus.shape, 1)
    turn, half = (-by) % LANES, (64 - by) % LANES
    p, m, h = (pltpu.roll(v, turn, 1) for v in (plus, minus, halo))
    m_half, h_half = pltpu.roll(minus, half, 1), pltpu.roll(halo, half, 1)
    if by > 0:
        ends, inner = lane >= LANES - by, (lane >= 64 - by) & (lane < 64)
    else:
        ends, inner = lane < -by, (lane >= 64) & (lane < 64 - by)
    return (
        jnp.where(ends, h, p),
        jnp.where(ends, h_half, m),
        jnp.where(ends, p, jnp.where(inner, m_half, h)),
    )


def halves(value):
    lane = lane_iota()
    turned = pltpu.roll(value, 64, 1)
    return jnp.where((lane < 32) | (lane >= 96), value + turned, turned - value)


def strip_tables(place, index, points, s):
    kinds = points[0].shape[1] // 2
    lane = lax.broadcasted_iota(jnp.int32, (2 * kinds, LANES), 1)
    kind = lax.broadcasted_iota(jnp.int32, (2 * kinds, LANES), 0)
    strips, groups = place[2], place[5]
    col = place[1]
    col_right = jnp.minimum(col + 1, groups - 1)
    col_left = jnp.maximum(col - 1, 0)
    at = jnp.clip(place[0] + s - 4, 0, strips - 1)
    own = index[at, col]
    side = jnp.where((lane & 32) == 0, index[at, col_right], index[at, col_left])
    side = jnp.where((lane < 32) | (lane >= 96), side, side + kinds)
    chosen = jnp.concatenate(
        [jnp.where(kind == v, 1.0, 0.0) for v in (own, own + kinds, side)], axis=1
    ).astype(jnp.bfloat16)
    parts = [jnp.dot(v, chosen, preferred_element_type=F32) for v in points]
    value = (parts[0] + parts[1]) + parts[2]
    return [value[:, q * LANES : (q + 1) * LANES] for q in range(3)]


def three_parts(value):
    high = value.astype(jnp.bfloat16)
    rest = value - high.astype(F32)
    middle = rest.astype(jnp.bfloat16)
    return high, middle, (rest - middle.astype(F32)).astype(jnp.bfloat16)


def adjoint_kernel(index, spread, tables_out, mark, tables, sems):
    place = whereabouts()
    points = three_parts(spread[...])
    mark[...] = jnp.zeros((8, LANES), F32)
    copies = []

    def send(n):
        copy = pltpu.make_async_copy(tables.at[n], tables_out.at[n], sems.at[n])
        copy.start()
        copies.append(copy)

    for s in range(9):
        values = strip_tables(place, index, points, s)
        if s == 4:
            for q in range(3):
                tables[9, q] = values[q]
            send(9)
        for b in range(SIDE):
            rows = slice(16 * b, 16 * b + 16)
            turned = shifted(*(v[rows] for v in values), REACH - b)
            for q in range(3):
                tables[s, q, rows, :] = turned[q]
        send(s)
    for copy in copies:
        copy.wait()


def forward_kernel(index, spread, after, tables):
    place = whereabouts()
    points = three_parts(spread[...])
    for s in range(5):
        values = strip_tables(place, index, points, s + 2)
        for q in range(3):
            tables[s, q] = values[q]


def table_copies(which, tables_in, tables, sems):
    for n, m in enumerate(which):
        pltpu.make_async_copy(tables_in.at[m], tables.at[n], sems.at[n]).start()

    def ready(n):
        pltpu.make_async_copy(tables_in.at[0], tables.at[n], sems.at[n]).wait()

    return ready


def operator_pass(
    count, place, resid, damping, tables, ready, forward, first_table, rolled, acc, rolled_two, image
):
    lane = lane_iota()
    row = row_iota()
    zero = jnp.zeros((8, LANES), F32)
    middle = count // 2

    for s in range(count):
        u0, u1, uh = (
            resid[s, n] * (1.0 / jnp.sqrt(resid[s, n] * resid[s, n] + damping)) for n in range(3)
        )
        base = (u0 + u1, u0 - u1, halves(uh))
        for b in range(SIDE):
            turned = shifted(*base, REACH - b)
            for q in range(3):
                rolled[b, q, 8 * s : 8 * s + 8, :] = turned[q]
    for q in range(3):
        for s in range(count + 2):
            acc[q, 8 * s : 8 * s + 8, :] = zero

    def back(taps, s):
        base = pl.multiple_of(8 * s, 8)
        ready(s)
        for q in range(3):
            sums = [None] * SIDE
            for b in range(SIDE):
                value = rolled[b, q, pl.ds(base, 8), :]
                for a in taps:
                    r = 16 * b + a
                    term = tables[s, q, r : r + 1, :] * value
                    sums[a] = term if sums[a] is None else sums[a] + term
            lo, mid, hi = zero, zero, zero
            for a in taps:
                m = a - REACH
                if m == 0:
                    mid = mid + sums[a]
                    continue
                turned = pltpu.roll(sums[a], m % 8, 0)
                if m > 0:
                    mid = mid + jnp.where(row >= m, turned, 0.0)
                    hi = hi + jnp.where(row < m, turned, 0.0)
                else:
                    mid = mid + jnp.where(row < 8 + m, turned, 0.0)
                    lo = lo + jnp.where(row >= 8 + m, turned, 0.0)
            for n, v in enumerate((lo, mid, hi)):
                at = pl.ds(pl.multiple_of(base + 8 * n, 8), 8)
                acc[q, at, :] = acc[q, at, :] + v

    for start, stop in ((0, 1), (1, count - 1), (count - 1, count)):
        taps = range(SIDE)
        if start == 0:
            taps = range(REACH + 1, SIDE)
        if stop == count:
            taps = range(REACH)

        def step(s, carry):
            back(taps, s)
            return carry

        lax.fori_loop(start, stop, step, 0)

    halo_ok = jnp.where((lane & 32) == 0, place[1] + 1, place[5] - place[1]) < place[5]
    descent = None
    for s in range(1, count - 1):
        at = place[0] + s - middle
        row_ok = jnp.where((at >= 0) & (at < place[2]), 1.0, 0.0)
        base = [acc[q, 8 * s + 8 : 8 * s + 16, :] * row_ok for q in range(3)]
        base[2] = jnp.where(halo_ok, base[2], 0.0)
        if s == middle:
            descent = base[:2]
        for b in range(SIDE):
            turned = shifted(*base, b - REACH)
            for q in range(3):
                rolled_two[b, q, 8 * s - 8 : 8 * s, :] = turned[q]

    def give(t, sums):
        at = place[0] + t - (count - 4) // 2
        row_ok = jnp.where((at >= 0) & (at < place[2]), 0.5, 0.0)
        plus, minus, halo = (v * row_ok for v in sums)
        image[t, 0] = plus + minus
        image[t, 1] = plus - minus
        image[t, 2] = jnp.where(halo_ok, halves(halo), 0.0)

    def taps_of(rows, base):
        for m in range(8):
            for b in range(SIDE):
                for q in range(3):
                    value = rolled_two[b, q, pl.ds(base + (m + 1), 8), :]
                    for t, low, sums in rows:
                        a = m if low else m + 8
                        if a < SIDE:
                            r = 16 * b + a
                            sums[q] = sums[q] + forward[first_table + t, q, r : r + 1, :] * value

    if first_table:
        ready(first_table)
    sums = [zero] * 3
    taps_of([(0, True, sums)], 0)

    def ahead(t, carry):
        old, new = list(carry), [zero] * 3
        taps_of([(t - 1, False, old), (t, True, new)], pl.multiple_of(8 * t, 8))
        give(t - 1, old)
        return tuple(new)

    sums = list(lax.fori_loop(1, count - 4, ahead, tuple(sums)))
    taps_of([(count - 5, False, sums)], 8 * (count - 4))
    give(count - 5, sums)
    plus, minus = descent
    return 0.5 * (plus + minus), 0.5 * (plus - minus)


def five_sums(descent, resid, image, middle, damping, payload):
    sums = [jnp.zeros((8, LANES), F32)] * 5
    for d in range(STEPS):
        g, r, q = descent[d], resid[middle, d], image[middle - 2, d]
        w = 1.0 / jnp.sqrt(r * r + damping)
        for n, v in enumerate((g * g, w * q * q, r * q, q * q, r * r)):
            sums[n] = sums[n] + v
    row = row_iota()
    packed = jnp.zeros((8, LANES), F32)
    for n in range(5):
        packed = jnp.where(row == n, jnp.sum(sums[n], axis=0, keepdims=True), packed)
    packed = jnp.sum(packed, axis=1, keepdims=True)
    lane = lane_iota()
    value = jnp.where((row == lane // 16) & (lane < 80), packed, 0.0)
    value = jnp.sum(value, axis=0, keepdims=True)
    for n in range(payload.shape[0]):
        payload[n] = value


def gathered(parts):
    sums = [parts[n, 0:1] for n in range(4)]
    for n in range(4, parts.shape[0]):
        sums[n % 4] = sums[n % 4] + parts[n, 0:1]
    return (sums[0] + sums[1]) + (sums[2] + sums[3])


def at_lane(total, spot):
    return total[:, spot : spot + 1]


def first_kernel(
    energies, near, beside, forward, tables_in, payload, state, descent, energy,
    strips, tables, sems, resid, image, rolled, acc, rolled_two,
):
    ready = table_copies(range(9), tables_in, tables, sems)
    place = whereabouts()
    total = at_lane(gathered(energies), ENERGY_LANE)
    energy[...] = jnp.broadcast_to(total, (1, LANES))
    damping = total / CELLS
    low = jnp.where(place[4] < 4, 0, GROUP)
    base = jnp.where(place[4] < 4, 4, 0)
    for n in range(4):
        strips[low + n] = beside[n]
    for n in range(GROUP):
        strips[base + n] = near[place[3] * GROUP + n]
    start = lax.rem(place[4], 4)
    for s in range(9):
        resid[s] = strips[start + s]
    pair = operator_pass(
        9, place, resid, damping, tables, ready, forward, 0, rolled, acc, rolled_two, image
    )
    for d in range(STEPS):
        descent[d] = pair[d]
    for s in range(5):
        state[s] = resid[s + 2]
        state[5 + s] = image[s]
    five_sums(pair, resid, image, 4, damping, payload)


def step_and_energy(parts, energy):
    total = gathered(parts)
    square, curve, cross, image, before = (at_lane(total, 16 * n) for n in range(5))
    step = square / curve
    start = before if energy is None else energy
    after = start - 2.0 * step * cross + step * step * image
    return step, jnp.maximum(after, 0.0)


def second_kernel(
    parts, energy, state, descent_in, tables_in, payload, descent, model,
    tables, sems, resid, image, rolled, acc, rolled_two,
):
    ready = table_copies((2, 3, 4, 5, 6, 9), tables_in, tables, sems)
    place = whereabouts()
    step, after = step_and_energy(parts, energy[:, 0:1])
    damping = after / CELLS
    for s in range(5):
        for d in range(3):
            resid[s, d] = state[s, d] - step * state[5 + s, d]
    for d in range(STEPS):
        model[d] = -(step * descent_in[d])

    pair = operator_pass(
        5, place, resid, damping, tables, ready, tables, 5, rolled, acc, rolled_two, image
    )
    for d in range(STEPS):
        descent[d] = pair[d]
    five_sums(pair, resid, image, 2, damping, payload)


def last_kernel(parts, descent, model, reflectivity, misfit):
    step, after = step_and_energy(parts, None)
    for d in range(STEPS):
        reflectivity[:, d, :] = model[d] - step * descent[d]
    misfit[...] = after / CELLS


def shape(*dims):
    return jax.ShapeDtypeStruct(dims, F32)


def all_sum(parts):
    near = lax.all_to_all(parts, NEAR, 0, 0)
    total = jnp.sum(near, axis=0)
    ways = SHAPE[0] * SHAPE[2]
    return lax.all_to_all(jnp.broadcast_to(total[None], (ways, 1, LANES)), FAR, 0, 0)


def local(receiver_field, source_field, velocity_class, filters, point_spread, spread_index):
    strips = SHAPE[2] * SHAPE[3] * SHAPE[4]
    groups = SHAPE[0] * SHAPE[1]
    columns = velocity_class.shape[1]
    chunks = columns // LANES
    scaling = 1.0 / math.sqrt(groups)
    blocks = chunks + chunks // 8
    landing = [
        pltpu.VMEM(receiver_field.shape, F32),
        pltpu.VMEM(source_field.shape, F32),
        pltpu.VMEM(velocity_class.shape, jnp.int32),
    ]
    inside, outside, given, kinds = pl.pallas_call(
        functools.partial(pack_kernel, chunks),
        out_shape=(
            shape(blocks, 8, LANES),
            shape(blocks, 8, LANES),
            shape(4, chunks, 8, LANES),
            jax.ShapeDtypeStruct((chunks, 8, LANES), jnp.int32),
        ),
        in_specs=[HBM] * 3,
        out_specs=tuple(whole(4)),
        scratch_shapes=landing + [pltpu.SemaphoreType.DMA((3,))],
        compiler_params=params(),
        name="pack",
    )(receiver_field, source_field, velocity_class)
    swaps = [(i, i ^ 1) for i in range(strips)]
    partner = lax.ppermute(inside, STRIP, swaps)
    crossings = [(i, i - 1 if i % 2 == 0 else i + 1) for i in range(1, strips - 1)]
    other = lax.ppermute(outside, STRIP, crossings)

    points = jnp.concatenate(
        [point_spread[:, 0] + point_spread[:, 1], point_spread[:, 0] - point_spread[:, 1]]
    ).transpose(2, 1, 0)
    points = jnp.pad(points, ((0, 0), (0, 1), (0, 0))).reshape(TAPS, -1)
    tables, mark = pl.pallas_call(
        adjoint_kernel,
        out_shape=(shape(24, 3, TAPS, LANES), shape(8, LANES)),
        in_specs=[SMEM] + whole(1),
        out_specs=(HBM, whole(1)[0]),
        scratch_shapes=[pltpu.VMEM((10, 3, TAPS, LANES), F32), pltpu.SemaphoreType.DMA((10,))],
        compiler_params=params(47),
        cost_estimate=pl.CostEstimate(flops=100000000, bytes_accessed=8000000, transcendentals=0),
        name="tables",
    )(spread_index, points)

    planes = chunks + 2
    one, two, edge, filt = pl.pallas_call(
        functools.partial(inner_kernel, chunks),
        out_shape=(
            shape(4, chunks, 8, LANES),
            shape(4, chunks, 8, LANES),
            shape(18, chunks, 8, LANES),
            shape(18, LANES),
        ),
        in_specs=whole(3),
        out_specs=tuple(whole(4)),
        scratch_shapes=[
            pltpu.VMEM((4, planes, 8, LANES), F32),
            pltpu.VMEM((4, chunks, 24, LANES), F32),
            pltpu.VMEM((4, chunks, 24, LANES), F32),
            pltpu.VMEM((4, chunks, 24, LANES), F32),
            pltpu.VMEM((18, chunks, 8, LANES), F32),
        ],
        compiler_params=params(),
        cost_estimate=pl.CostEstimate(flops=100000000, bytes_accessed=8000000, transcendentals=0),
        name="inner",
    )(given, kinds, filters)
    terms = pl.pallas_call(
        functools.partial(edge_kernel, chunks),
        out_shape=shape(chunks, 3, 8, LANES),
        in_specs=whole(8),
        out_specs=whole(1)[0],
        scratch_shapes=[
            pltpu.VMEM((5, planes, 8, LANES), F32),
            pltpu.VMEM((STEPS, planes, 8, LANES), F32),
        ],
        compiler_params=params(),
        name="edges",
    )(filt, one, two, edge, inside, outside, partner, other)
    terms = lax.all_to_all(terms, FREQ, 0, 0)

    nearby = SHAPE[1] * SHAPE[3] * SHAPE[4]
    far = SHAPE[0] * SHAPE[2]
    migrated, payload = pl.pallas_call(
        functools.partial(sum_kernel, scaling),
        out_shape=(shape(8, STEPS, LANES), shape(nearby, 3, 8, LANES)),
        in_specs=whole(2),
        out_specs=tuple(whole(2)),
        compiler_params=params(),
        name="stack",
    )(terms, mark)
    near = lax.all_to_all(payload, NEAR, 0, 0)
    energies, beside = pl.pallas_call(
        relay_kernel,
        out_shape=(shape(far, 2, LANES), shape(4, 3, 8, LANES)),
        in_specs=whole(1),
        out_specs=tuple(whole(2)),
        compiler_params=params(),
        name="relay",
    )(near)
    exchanged = lax.all_to_all(energies, FAR, 0, 0)
    pairs = []
    for i in range(strips):
        to = i + GROUP if i % GROUP < 4 else i - GROUP
        if 0 <= to < strips:
            pairs.append((i, to))
    beside = lax.ppermute(beside, STRIP, pairs)
    forward = pl.pallas_call(
        forward_kernel,
        out_shape=shape(5, 3, TAPS, LANES),
        in_specs=[SMEM] + whole(2),
        out_specs=whole(1)[0],
        compiler_params=params(),
        cost_estimate=pl.CostEstimate(flops=100000000, bytes_accessed=8000000, transcendentals=0),
        name="ahead",
    )(spread_index, points, energies)

    def scratch(count):
        return [
            pltpu.VMEM((count, 3, 8, LANES), F32),
            pltpu.VMEM((count - 4, 3, 8, LANES), F32),
            pltpu.VMEM((SIDE, 3, 8 * count, LANES), F32),
            pltpu.VMEM((3, 8 * count + 16, LANES), F32),
            pltpu.VMEM((SIDE, 3, 8 * count - 16, LANES), F32),
        ]

    parts, state, descent, energy = pl.pallas_call(
        first_kernel,
        out_shape=(
            shape(nearby, 1, LANES),
            shape(10, 3, 8, LANES),
            shape(STEPS, 8, LANES),
            shape(1, LANES),
        ),
        in_specs=whole(4) + [HBM],
        out_specs=tuple(whole(4)),
        scratch_shapes=[
            pltpu.VMEM((12, 3, 8, LANES), F32),
            pltpu.VMEM((9, 3, TAPS, LANES), F32),
            pltpu.SemaphoreType.DMA((9,)),
        ]
        + scratch(9),
        compiler_params=params(47),
        name="pass_one",
    )(exchanged, near, beside, forward, tables)
    parts = all_sum(parts)
    parts, descent, model = pl.pallas_call(
        second_kernel,
        out_shape=(shape(nearby, 1, LANES), shape(STEPS, 8, LANES), shape(STEPS, 8, LANES)),
        in_specs=whole(4) + [HBM],
        out_specs=tuple(whole(3)),
        scratch_shapes=[pltpu.VMEM((6, 3, TAPS, LANES), F32), pltpu.SemaphoreType.DMA((6,))]
        + scratch(5),
        compiler_params=params(47),
        name="pass_two",
    )(parts, energy, state, descent, tables)
    parts = all_sum(parts)
    reflectivity, misfit = pl.pallas_call(
        last_kernel,
        out_shape=(shape(8, STEPS, LANES), shape(1, 1)),
        in_specs=whole(3),
        out_specs=tuple(whole(2)),
        compiler_params=params(),
        name="last",
    )(parts, descent, model)
    return migrated, reflectivity, misfit.reshape(())


def solution(mesh):
    fine = Mesh(mesh.devices.reshape(SHAPE), NAMES)
    return jax.shard_map(
        local,
        mesh=fine,
        in_specs=(
            P(None, FREQ, STRIP, None),
            P(None, FREQ, STRIP, None),
            P(STRIP, None),
            P(FREQ, None, None, None),
            P(),
            P(),
        ),
        out_specs=(P(STRIP, None, FREQ), P(STRIP, None, FREQ), P()),
        check_vma=False,
    )
```
